256 devices in a mesh: dp: 16 (over y, x), tensor: 16 (over z, core).
Axes of the slice: x: 4, y: 4, z: 8, core: 2. Of those that a mesh axis runs over, the one named last changes fastest.
Arguments:
- head_out: bfloat16 [1024, 8192], P('dp', 'tensor'), may hold values from -9 to 9
- residual: bfloat16 [1024, 8192], P('tensor', 'dp'), may hold values from -9 to 9
- class_ids: int32 [1024], replicated, may hold values from 0 to 255
- head_mask: int32 [64], P('tensor'), may hold values 0 or 1
- out_weight: bfloat16 [8192, 8192], P('tensor', 'dp'), may hold values from -0.0625 to 0.0625
- norm_gain: bfloat16 [8192], P('dp'), may hold values from 0.5 to 1.5
- gate_up: bfloat16 [8192, 2, 14336], P('dp', None, 'tensor'), may hold values from -0.0625 to 0.0625
- down_weight: bfloat16 [14336, 8192], P('tensor', 'dp'), may hold values from -0.046875 to 0.046875
Outputs:
- layer_out: bfloat16 [1024, 8192], P('tensor', 'dp')
The draws below stay inside these ranges and needn't reach their ends.
All inputs are finite; a program needn't handle non-finite values. No bound on the sum of `head_mask` on one device may be relied on, other than what follows from the above.
Results may differ from the reference program's by a relative error of at most 0.0066.
Values may be sent and summed in bfloat16 or wider, within the bound.
A program may use at most 64 MiB of HBM per device.

```python
import math
import jax
import jax.numpy as jnp
import numpy as np
from jax import lax

D = 8192
HEADS = 64
HEAD_DIM = 128
FF = 14336
CLASSES = 256
TOKENS = 1024


def scale_grid(key, rows, cols, row_low, row_high, col_low, col_high):
    row_key, col_key = jax.random.split(key)
    row_scale = jnp.exp(jax.random.uniform(row_key, (rows, 1), jnp.float32, math.log(row_low), math.log(row_high)))
    col_scale = jnp.exp(jax.random.uniform(col_key, (1, cols), jnp.float32, math.log(col_low), math.log(col_high)))
    return row_scale * col_scale


def spread_rows(key, rows, cols):
    noise_key = jax.random.fold_in(key, 0)
    grid_key = jax.random.fold_in(key, 2)
    noise_part = jax.random.truncated_normal(noise_key, -4.0, 4.0, (rows, cols), jnp.float32)
    values = noise_part * scale_grid(grid_key, rows, cols, 0.15, 1.5, 0.15, 1.5)
    return values.astype(jnp.bfloat16)


def draw_head_out(key, part):
    key = jax.random.fold_in(key, 7)
    return spread_rows(key, TOKENS, HEADS * HEAD_DIM)


def draw_residual(key, part):
    key = jax.random.fold_in(key, 13)
    return spread_rows(key, TOKENS, D)


def with_ends(array, stream_key, smallest, high):
    shape = array.shape
    index_at = [jax.random.randint(jax.random.fold_in(stream_key, axis), (), 0, shape[axis]) for axis in range(len(shape))]
    array = array.at[tuple(index_at)].set(smallest)
    longest = shape.index(max(shape))
    index_at[longest] = (index_at[longest] + 1) % shape[longest]
    return array.at[tuple(index_at)].set(high)


def block_levels(stream_key, dims, cuts, low, top_value):
    def one(dim, blocks):
        draws = jax.random.uniform(jax.random.fold_in(jax.random.fold_in(stream_key, 6), dim), (blocks,), jnp.float32, low / len(cuts), top_value / len(cuts))
        return jnp.repeat(jnp.exp(draws), dims[dim] // blocks).reshape((-1,) + (1,) * (len(dims) - dim - 1))

    gain = one(*cuts[0])
    for cut in cuts[1:]:
        gain = gain * one(*cut)
    return gain


def cumulative_ranks(count, skew):
    weights = [(1 << 20) // math.isqrt(standing ** skew) + 1 for standing in range(1, count + 1)]
    width = 1 + sum(weights) // (1 << 30)
    return np.cumsum(np.array([max(1, weight // width) for weight in weights]))


def ranked(stream_key, dims, number_of, slope):
    listing = cumulative_ranks(number_of, slope)
    lot = jax.random.randint(jax.random.fold_in(stream_key, 1), dims, 0, int(listing[number_of - 1]))
    rank = jnp.searchsorted(jnp.asarray(listing, jnp.int32), lot, side="right")
    return jax.random.permutation(jax.random.fold_in(stream_key, 2), number_of)[rank].astype(jnp.int32)


def scatter_about(rng, dims, scale, bound, pieces=(), held_as=jnp.bfloat16):
    entries = jax.random.normal(rng, dims, jnp.float32) * scale
    if len(pieces) > 0:
        entries = block_levels(rng, dims, pieces, -0.22, 0.18) * entries
    return jnp.clip(entries, min=-bound, max=bound).astype(held_as)


def setup_inputs(seed: int = 0) -> dict:
    key_of = jax.random.split(jax.random.key(seed), 9)
    head_out = draw_head_out(jax.random.fold_in(key_of[8], 71), 0)
    residual = draw_residual(jax.random.fold_in(key_of[8], 71), 0)
    class_ids = with_ends(ranked(key_of[2], (TOKENS,), CLASSES, 2), jax.random.fold_in(key_of[2], 3), 0, CLASSES - 1).astype(jnp.int32)
    head_mask = with_ends((jax.random.randint(key_of[3], (HEADS,), 0, 2) < 1).astype(jnp.int32), jax.random.fold_in(key_of[3], 1), 0, 1)
    out_weight = scatter_about(key_of[4], (HEADS * HEAD_DIM, D), (HEADS * HEAD_DIM) ** -0.5, 0.0625, ((0, 16), (1, 16)))
    norm_gain = jnp.clip(1.0 + 0.1 * jax.random.normal(key_of[5], (D,), jnp.float32), 0.5, 1.5).astype(jnp.bfloat16)
    gate_up = scatter_about(key_of[6], (D, 2, FF), D ** -0.5, 0.0625, ((0, 16), (2, 16)))
    down_weight = scatter_about(key_of[7], (FF, D), FF ** -0.5, 0.046875, ((0, 16), (1, 16)))
    return {"head_out": head_out, "residual": residual, "class_ids": class_ids, "head_mask": head_mask, "out_weight": out_weight, "norm_gain": norm_gain, "gate_up": gate_up, "down_weight": down_weight}


norm_eps = 1e-05

def reference(head_out, residual, class_ids, head_mask, out_weight, norm_gain, gate_up, down_weight):
    classes = jnp.arange(CLASSES, dtype=jnp.int32)
    onehot = (class_ids[:, None] == classes[None, :]).astype(jnp.bfloat16)
    totals = lax.dot_general(onehot, head_out, (((0,), (0,)), ((), ())), preferred_element_type=jnp.float32)
    counts = lax.optimization_barrier(jnp.sum(onehot.astype(jnp.float32), axis=0))
    class_means = (totals / jnp.maximum(counts, 1.0)[:, None]).astype(jnp.bfloat16)
    looked = jnp.dot(onehot, class_means, preferred_element_type=jnp.float32).astype(jnp.bfloat16)
    ablate = jnp.repeat(head_mask, HEAD_DIM) == 1
    patched = jnp.where(ablate[None, :], looked, head_out)
    attended = jnp.dot(patched, out_weight, preferred_element_type=jnp.float32)
    stream = (residual.astype(jnp.float32) + attended).astype(jnp.bfloat16)
    stream_wide = stream.astype(jnp.float32)
    squares = lax.optimization_barrier(jnp.sum(stream_wide * stream_wide, axis=1))
    inverse = lax.rsqrt(squares / D + norm_eps)
    scaled = (stream_wide * norm_gain.astype(jnp.float32)[None, :]).astype(jnp.bfloat16)
    projection = jnp.dot(scaled, gate_up.reshape(D, 2 * FF), preferred_element_type=jnp.float32)
    gate_part = projection[:, :FF] * inverse[:, None]
    up_part = projection[:, FF:] * inverse[:, None]
    hidden = (jax.nn.silu(gate_part) * up_part).astype(jnp.bfloat16)
    lowered = jnp.dot(hidden, down_weight, preferred_element_type=jnp.float32)
    return (stream_wide + lowered).astype(jnp.bfloat16)
```

```python
import functools

import jax
import jax.numpy as jnp
from jax import lax
from jax.experimental import pallas as pl
from jax.experimental.pallas import tpu as pltpu
from jax.sharding import PartitionSpec as P

MESH = pl.DeviceIdType.MESH
BF16 = jnp.bfloat16
F32 = jnp.float32
D = 8192
HEAD_DIM = 128
CLASSES = 256
EPS = 1e-05
TOKENS = 1024
W = 512
FF = 896
NQ = 2
R = 64 // NQ
ORDERS = ((3, 2, 1, 0), (2, 3, 0, 1), (1, 0, 3, 2), (0, 1, 2, 3))
D_WIDTH = (512, 512, 512, 384)
E_WIDTH = (256, 256, 256, 128)


def dot(a, b):
    return jnp.dot(a, b, preferred_element_type=F32)


def kernel(ho, res, ids, mask, ow, gain, gu, dw, out,
           ow_v, gu_v, dw_v, res_v, g, oh, oht, a, ar, az, st, p, r1, r2, r3, r4, h0, h1, h2, h3, f, fr, fz,
           load_sem, a_s, a_r, b_s, b_r, bz_s, bz_r, cz_s, cz_r, c_s, c_r, d_s, d_r, e_s, e_r, f_s, f_r, fz_s, fz_r):
    dp = lax.axis_index("dp")
    tn = lax.axis_index("tensor")
    y, x = dp // 4, dp % 4
    z, c = tn // 2, tn % 2
    rs = (r1, r2, r3, r4)
    hs = (h0, h1, h2, h3)
    bits = (y // 2, (y + y // 2) % 2, x // 2, (x + x // 2) % 2)
    near = (
        ((3 - y) * 4 + x, tn),
        ((y + 1 - 2 * (y % 2)) * 4 + x, tn),
        (y * 4 + 3 - x, tn),
        (y * 4 + x + 1 - 2 * (x % 2), tn),
    )
    sibling = (dp, z * 2 + 1 - c)

    def x_peer(k):
        return (y * 4 + (x + k) % 4, tn)

    def y_peer(k):
        return (((y + k) % 4) * 4 + x, tn)

    def z_peer(k):
        return (dp, ((z + k) % 8) * 2 + c)

    sends = []

    def send(src, dst, ssem, rsem, to):
        cp = pltpu.make_async_remote_copy(src_ref=src, dst_ref=dst, send_sem=ssem, recv_sem=rsem,
                                          device_id=to, device_id_type=MESH)
        cp.start()
        sends.append(cp)

    def arrived(ref, ssem, rsem):
        pltpu.make_async_remote_copy(src_ref=ref, dst_ref=ref, send_sem=ssem, recv_sem=rsem,
                                     device_id=sibling, device_id_type=MESH).wait_recv()

    loads = [
        pltpu.make_async_copy(ho.at[:, 0:256], g.at[0, y, x], load_sem.at[0]),
        pltpu.make_async_copy(ho.at[:, 256:512], g.at[1, y, x], load_sem.at[1]),
        pltpu.make_async_copy(ow, ow_v, load_sem.at[2]),
        pltpu.make_async_copy(gu, gu_v, load_sem.at[3]),
        pltpu.make_async_copy(dw, dw_v, load_sem.at[4]),
        pltpu.make_async_copy(res, res_v, load_sem.at[5]),
    ]
    for cp in loads:
        cp.start()

    barrier = pltpu.get_barrier_semaphore()
    peers = [x_peer(k) for k in (1, 2, 3)] + [y_peer(k) for k in (1, 2, 3)] + [z_peer(k) for k in range(1, 8)] + [sibling]
    for to in peers:
        pl.semaphore_signal(barrier, inc=1, device_id=to, device_id_type=MESH)
    pl.semaphore_wait(barrier, len(peers))

    loads[0].wait()
    loads[1].wait()
    for k in (1, 2, 3):
        send(g.at[0, y, x], g.at[0, y, x], a_s.at[0, k - 1], a_r.at[0, k - 1], x_peer(k))
        send(g.at[1, y, x], g.at[1, y, x], a_s.at[1, k - 1], a_r.at[1, k - 1], y_peer(k))
    ids_row = ids[...]
    same = lax.broadcasted_iota(jnp.int32, (CLASSES, TOKENS), 0) == ids_row
    onehot = same.astype(F32)
    counts = jnp.sum(onehot, axis=1, keepdims=True)
    oh[...] = onehot.astype(BF16)
    oht[...] = onehot.T.astype(BF16)
    for k in (1, 2, 3):
        arrived(g.at[0, y, x], a_s.at[0, k - 1], a_r.at[0, k - 1])
        arrived(g.at[1, y, x], a_s.at[1, k - 1], a_r.at[1, k - 1])
    for k in (1, 2, 3):
        send(g.at[0, y], g.at[0, y], a_s.at[2, k - 1], a_r.at[2, k - 1], y_peer(k))
        send(g.at[1, :, x], g.at[1, :, x], a_s.at[3, k - 1], a_r.at[3, k - 1], x_peer(k))
    for k in (1, 2, 3):
        arrived(g.at[0, y], a_s.at[2, k - 1], a_r.at[2, k - 1])
        arrived(g.at[1, :, x], a_s.at[3, k - 1], a_r.at[3, k - 1])

    means = []
    for h in (0, 1):
        totals = dot(oh[...], g[h].reshape(TOKENS, 256))
        means.append((totals / jnp.maximum(counts, 1.0)).astype(BF16))
    lane_head = lax.broadcasted_iota(jnp.int32, (1, 256), 1) // HEAD_DIM
    ablate = [jnp.where(lane_head == 0, mask[2 * h], mask[2 * h + 1]) == 1 for h in (0, 1)]
    loads[2].wait()
    for i in range(4):
        rows = oht[256 * i:256 * i + 256]
        total = None
        for h in (0, 1):
            looked = dot(rows, means[h])
            patched = jnp.where(ablate[h], looked, g[h, i].reshape(256, 256).astype(F32)).astype(BF16)
            part = dot(patched, ow_v[256 * h:256 * h + 256])
            total = part if total is None else total + part
        a[2 * i:2 * i + 2] = total.astype(BF16).reshape(2, 2, 64, W)

    def rows_of(q):
        return pl.ds(R * q, R)

    def pair_send(q, buf, recv, ssem, rsem):
        send(buf.at[:, 1 - c, rows_of(q)], recv.at[q], ssem.at[q], rsem.at[q], sibling)

    def ring_send(q, buf, recv, ssem, rsem, zrecv, zs, zr):
        arrived(recv.at[q], ssem.at[q], rsem.at[q])
        both = buf[:, c, rows_of(q)].astype(F32) + recv[q].astype(F32)
        buf[:, c, rows_of(q)] = both.astype(BF16)
        for k in (4, 3, 5, 2, 6, 1, 7):
            send(buf.at[(z + k) % 8, c, rows_of(q)], zrecv.at[q, k], zs.at[q, k], zr.at[q, k], z_peer(k))

    def ring_total(q, buf, zrecv, zs, zr):
        total = buf[z, c, rows_of(q)].astype(F32)
        for k in (1, 7, 2, 6, 3, 5, 4):
            arrived(zrecv.at[q, k], zs.at[q, k], zr.at[q, k])
            total = total + zrecv[q, k].astype(F32)
        return total

    def b1(q):
        pair_send(q, a, ar, b_s, b_r)

    def b2(q):
        ring_send(q, a, ar, b_s, b_r, az, bz_s, bz_r)

    def c1(q):
        if q == 0:
            loads[5].wait()
        stream = res_v[rows_of(q)].astype(F32) + ring_total(q, a, az, bz_s, bz_r)
        st[z, c, rows_of(q)] = stream.astype(BF16)
        mine = st.at[z, c, rows_of(q)]
        for k in (4, 3, 5, 2, 6, 1, 7):
            send(mine, mine, cz_s.at[q, k], cz_r.at[q, k], z_peer(k))

    def c2(q):
        mine = st.at[z, c, rows_of(q)]
        for k in (1, 7, 2, 6, 3, 5, 4):
            arrived(mine, cz_s.at[q, k], cz_r.at[q, k])
        col = st.at[:, c, rows_of(q)]
        send(col, col, c_s.at[q], c_r.at[q], sibling)

    def cube(i, order, step, flip):
        at = [slice(None)] * 4
        for n in range(step):
            at[order[n]] = bits[order[n]]
        if flip:
            at[order[step]] = 1 - bits[order[step]]
        return tuple(at)

    def d_send(q, i, step):
        order = ORDERS[i]
        at = cube(i, order, step, True)
        if step > 0:
            total = p[(q, i) + at].astype(F32)
            for n in range(step):
                total = total + rs[n][(q, i) + at].astype(F32)
            p[(q, i) + at] = total.astype(BF16)
        lanes = (slice(None),) + (pl.ds(0, D_WIDTH[i]),)
        where = (q, i) + at + lanes
        send(p.at[where], rs[step].at[where], d_s.at[q, i, step], d_r.at[q, i, step], near[order[step]])

    def d_arrived(q, i, step):
        order = ORDERS[i]
        at = list(cube(i, order, step, False))
        at[order[step]] = bits[order[step]]
        lanes = (slice(None),) + (pl.ds(0, D_WIDTH[i]),)
        arrived(rs[step].at[(q, i) + tuple(at) + lanes], d_s.at[q, i, step], d_r.at[q, i, step])

    def d1(q):
        if q == 0:
            loads[3].wait()
        col = st.at[:, 1 - c, rows_of(q)]
        arrived(col, c_s.at[q], c_r.at[q])
        wide = st[:, :, rows_of(q)].reshape(16 * R, W).astype(F32)
        squares = jnp.sum(wide * wide, axis=1, keepdims=True)
        scaled = (wide * gain[...].astype(F32)).astype(BF16)
        for i in range(4):
            width = 512 if i < 3 else 256
            part = dot(scaled, gu_v[:, 512 * i:512 * i + width]).astype(BF16)
            p[q, i, :, :, :, :, :, 0:width] = part.reshape(2, 2, 2, 2, R, width)
            if i == 3:
                wide_squares = jnp.broadcast_to(squares, (16 * R, 128)).astype(BF16)
                p[q, i, :, :, :, :, :, 256:384] = wide_squares.reshape(2, 2, 2, 2, R, 128)
            d_send(q, i, 0)

    def d_next(q, step):
        for i in range(4):
            d_arrived(q, i, step - 1)
            d_send(q, i, step)

    def e_ref(q, i, step):
        order = ORDERS[i]
        at = [slice(None)] * 4
        for n in range(4 - step):
            at[order[n]] = bits[order[n]]
        return tuple(at)

    def e_send(q, i, step):
        where = (q,) + e_ref(q, i, step)
        dim = ORDERS[i][3 - step]
        send(hs[i].at[where], hs[i].at[where], e_s.at[q, i, step], e_r.at[q, i, step], near[dim])

    def e_arrived(q, i, step):
        at = list(e_ref(q, i, step))
        dim = ORDERS[i][3 - step]
        at[dim] = 1 - bits[dim]
        arrived(hs[i].at[(q,) + tuple(at)], e_s.at[q, i, step], e_r.at[q, i, step])

    def d5(q):
        sums = []
        for i in range(4):
            d_arrived(q, i, 3)
            at = (q, i) + tuple(bits)
            total = p[at].astype(F32)
            for n in range(4):
                total = total + rs[n][at].astype(F32)
            sums.append(total)
        inverse = lax.rsqrt(sums[3][:, 256:384] / D + EPS)

        def tile(n):
            return sums[n // 4][:, 128 * (n % 4):128 * (n % 4) + 128] * inverse

        for i in range(4):
            for n in range(E_WIDTH[i] // 128):
                gate, up = tile(2 * i + n), tile(7 + 2 * i + n)
                hidden = gate / (1.0 + jnp.exp(-gate)) * up
                hs[i][(q,) + tuple(bits) + (slice(None), slice(128 * n, 128 * n + 128))] = hidden.astype(BF16)
            e_send(q, i, 0)

    def e_next(q, step):
        for i in range(4):
            e_arrived(q, i, step - 1)
            e_send(q, i, step)

    def f1(q):
        if q == 0:
            loads[4].wait()
        total = None
        for i in range(4):
            e_arrived(q, i, 3)
            part = dot(hs[i][q].reshape(16 * R, E_WIDTH[i]), dw_v[256 * i:256 * i + E_WIDTH[i]])
            total = part if total is None else total + part
        f[:, :, rows_of(q)] = total.astype(BF16).reshape(8, 2, R, W)
        pair_send(q, f, fr, f_s, f_r)

    def f2(q):
        ring_send(q, f, fr, f_s, f_r, fz, fz_s, fz_r)

    def f3(q):
        total = st[z, c, rows_of(q)].astype(F32) + ring_total(q, f, fz, fz_s, fz_r)
        out[rows_of(q)] = total.astype(BF16)

    stages = [b1, b2, c1, c2, d1]
    stages += [functools.partial(d_next, step=s) for s in (1, 2, 3)] + [d5]
    stages += [functools.partial(e_next, step=s) for s in (1, 2, 3)] + [f1, f2, f3]
    for stage in stages:
        for q in range(NQ):
            stage(q)
    for cp in sends:
        cp.wait_send()


def local(head_out, residual, class_ids, head_mask, out_weight, norm_gain, gate_up, down_weight):
    hbm = pl.BlockSpec(memory_space=pl.ANY)
    vmem = pl.BlockSpec(memory_space=pltpu.VMEM)
    smem = pl.BlockSpec(memory_space=pltpu.SMEM)
    dma = pltpu.SemaphoreType.DMA
    cube = (NQ, 4, 2, 2, 2, 2, R, 512)
    return pl.pallas_call(
        kernel,
        out_shape=jax.ShapeDtypeStruct((64, W), BF16),
        in_specs=[hbm, hbm, vmem, smem, hbm, vmem, hbm, hbm],
        out_specs=vmem,
        scratch_shapes=[
            pltpu.VMEM((W, W), BF16),
            pltpu.VMEM((W, 2 * FF), BF16),
            pltpu.VMEM((FF, W), BF16),
            pltpu.VMEM((64, W), BF16),
            pltpu.VMEM((2, 4, 4, 64, 256), BF16),
            pltpu.VMEM((CLASSES, TOKENS), BF16),
            pltpu.VMEM((TOKENS, CLASSES), BF16),
            pltpu.VMEM((8, 2, 64, W), BF16),
            pltpu.VMEM((NQ, 8, R, W), BF16),
            pltpu.VMEM((NQ, 8, R, W), BF16),
            pltpu.VMEM((8, 2, 64, W), BF16),
            pltpu.VMEM(cube, BF16), pltpu.VMEM(cube, BF16), pltpu.VMEM(cube, BF16),
            pltpu.VMEM(cube, BF16), pltpu.VMEM(cube, BF16),
            *[pltpu.VMEM((NQ, 2, 2, 2, 2, R, w), BF16) for w in E_WIDTH],
            pltpu.VMEM((8, 2, 64, W), BF16),
            pltpu.VMEM((NQ, 8, R, W), BF16),
            pltpu.VMEM((NQ, 8, R, W), BF16),
            dma((6,)),
            dma((4, 3)), dma((4, 3)),
            dma((NQ,)), dma((NQ,)),
            dma((NQ, 8)), dma((NQ, 8)),
            dma((NQ, 8)), dma((NQ, 8)),
            dma((NQ,)), dma((NQ,)),
            dma((NQ, 4, 4)), dma((NQ, 4, 4)),
            dma((NQ, 4, 4)), dma((NQ, 4, 4)),
            dma((NQ,)), dma((NQ,)),
            dma((NQ, 8)), dma((NQ, 8)),
        ],
        compiler_params=pltpu.CompilerParams(
            collective_id=0, has_side_effects=True, vmem_limit_bytes=56 << 20
        ),
        name="layer",
    )(head_out, residual, class_ids.reshape(1, TOKENS), head_mask, out_weight, norm_gain.reshape(1, W),
      gate_up.reshape(W, 2 * FF), down_weight)


def solution(mesh):
    in_specs = (
        P("dp", "tensor"),
        P("tensor", "dp"),
        P(),
        P("tensor"),
        P("tensor", "dp"),
        P("dp"),
        P("dp", None, "tensor"),
        P("tensor", "dp"),
    )
    return jax.shard_map(local, mesh=mesh, in_specs=in_specs, out_specs=P("tensor", "dp"), check_vma=False)
```

```python
import functools

import jax
import jax.numpy as jnp
from jax import lax
from jax.experimental import pallas as pl
from jax.experimental.pallas import tpu as pltpu
from jax.sharding import PartitionSpec as P

MESH = pl.DeviceIdType.MESH
BF16 = jnp.bfloat16
F32 = jnp.float32
D = 8192
HEAD_DIM = 128
CLASSES = 256
EPS = 1e-05
TOKENS = 1024
W = 512
FF = 896
NQ = 2
R = 64 // NQ
RD = R // 2
ORDERS = ((3, 2, 1, 0), (2, 3, 0, 1), (1, 0, 3, 2), (0, 1, 2, 3))
E_TILES = ((0, 4), (4, 8), (8, 11), (11, 14))


def dot(a, b):
    return jnp.dot(a, b, preferred_element_type=F32)


def kernel(ho, res, ids, mask, ow, gain, gu, dw, out,
           ow_v, gu_in, gu_v, dw_v, res_v, g, oh, oht, a, ar, az, azh, ah, st, p, r1, r2, r3, r4, h0, h1, h2, h3, f, fz, fzh,
           load_sem, w_s, w_r, x_s, x_r, a_s, a_r, b_s, b_r, bz_s, bz_r, cz_s, cz_r, d_s, d_r, e_s, e_r, fz_s, fz_r):
    dp = lax.axis_index("dp")
    tn = lax.axis_index("tensor")
    y, x = dp // 4, dp % 4
    z, c = tn // 2, tn % 2
    rs = (r1, r2, r3, r4)
    hs = (h0, h1, h2, h3)
    bits = (y // 2, (y + y // 2) % 2, x // 2, (x + x // 2) % 2)
    near = (
        ((3 - y) * 4 + x, tn),
        ((y + 1 - 2 * (y % 2)) * 4 + x, tn),
        (y * 4 + 3 - x, tn),
        (y * 4 + x + 1 - 2 * (x % 2), tn),
    )
    sibling = (dp, z * 2 + 1 - c)

    def x_peer(k):
        return (y * 4 + (x + k) % 4, tn)

    def y_peer(k):
        return (((y + k) % 4) * 4 + x, tn)

    def z_peer(k):
        return (dp, ((z + k + 8) % 8) * 2 + c)

    def block(k):
        return (z + k + 8) % 8

    sends = []

    def send(src, dst, ssem, rsem, to):
        cp = pltpu.make_async_remote_copy(src_ref=src, dst_ref=dst, send_sem=ssem, recv_sem=rsem,
                                          device_id=to, device_id_type=MESH)
        cp.start()
        sends.append(cp)

    def arrived(ref, ssem, rsem):
        pltpu.make_async_remote_copy(src_ref=ref, dst_ref=ref, send_sem=ssem, recv_sem=rsem,
                                     device_id=sibling, device_id_type=MESH).wait_recv()

    loads = [
        pltpu.make_async_copy(ho.at[:, 0:256], g.at[0, y, x], load_sem.at[0]),
        pltpu.make_async_copy(ho.at[:, 256:512], g.at[1, y, x], load_sem.at[1]),
        pltpu.make_async_copy(gu, gu_in, load_sem.at[2]),
        pltpu.make_async_copy(dw, dw_v.at[0], load_sem.at[3]),
        pltpu.make_async_copy(ow, ow_v, load_sem.at[4]),
        pltpu.make_async_copy(res, res_v, load_sem.at[5]),
    ]
    for cp in loads:
        cp.start()

    barrier = pltpu.get_barrier_semaphore()
    peers = [x_peer(k) for k in (1, 2, 3)] + [y_peer(k) for k in (1, 2, 3)] + [z_peer(k) for k in (1, -1, 2, -2)] + [sibling]
    for to in peers:
        pl.semaphore_signal(barrier, inc=1, device_id=to, device_id_type=MESH)

    loads[2].wait()
    gu_v[0] = gu_in[:, 0, :]
    gu_v[1] = gu_in[:, 1, :]
    same = lax.broadcasted_iota(jnp.int32, (CLASSES, TOKENS), 0) == ids[...]
    onehot = same.astype(F32)
    counts = jnp.sum(onehot, axis=1, keepdims=True)
    oh[...] = onehot.astype(BF16)
    oht[...] = onehot.T.astype(BF16)
    loads[0].wait()
    loads[1].wait()
    loads[3].wait()
    pl.semaphore_wait(barrier, len(peers))

    first = ((x_peer, y_peer), (y_peer, x_peer))
    for k in (1, 3, 2):
        for h in (0, 1):
            send(g.at[h, y, x], g.at[h, y, x], x_s.at[h, k], x_r.at[h, k], first[h][0](k))
    for k in (1, 3, 2):
        for h in (0, 1):
            send(g.at[h, y, x], g.at[h, y, x], a_s.at[h, 0, k], a_r.at[h, 0, k], first[h][1](k))
    send(gu_v.at[0:2], gu_v.at[2:4], w_s.at[0], w_r.at[0], sibling)
    send(dw_v.at[0], dw_v.at[1], w_s.at[1], w_r.at[1], sibling)
    for j in (1, 3, 2):
        for h in (0, 1):
            got = g.at[h, y, (x - j + 4) % 4] if h == 0 else g.at[h, (y - j + 4) % 4, x]
            arrived(got, x_s.at[h, j], x_r.at[h, j])
            for k in (1, 3, 2):
                send(got, got, a_s.at[h, j, k], a_r.at[h, j, k], first[h][1](k))
    for j in range(4):
        for k in (1, 2, 3):
            for h in (0, 1):
                arrived(g.at[h, y, x], a_s.at[h, j, k], a_r.at[h, j, k])

    means = []
    for h in (0, 1):
        totals = dot(oh[...], g[h].reshape(TOKENS, 256))
        means.append((totals / jnp.maximum(counts, 1.0)).astype(BF16))
    lane_head = lax.broadcasted_iota(jnp.int32, (1, 256), 1) // HEAD_DIM
    ablate = [jnp.where(lane_head == 0, mask[2 * h], mask[2 * h + 1]) == 1 for h in (0, 1)]
    loads[4].wait()
    for i in range(4):
        rows = oht[256 * i:256 * i + 256]
        total = None
        for h in (0, 1):
            looked = dot(rows, means[h])
            patched = jnp.where(ablate[h], looked, g[h, i].reshape(256, 256).astype(F32)).astype(BF16)
            part = dot(patched, ow_v[256 * h:256 * h + 256])
            total = part if total is None else total + part
        a[2 * i:2 * i + 2] = total.astype(BF16).reshape(2, 2, 64, W)

    def rows_of(q):
        return pl.ds(R * q, R)

    def z_first(q, buf, recv, half, ss, sr):
        r = rows_of(q)
        low, high = pl.ds(R * q, R // 2), pl.ds(R * q + R // 2, R // 2)
        send(buf.at[block(3), r], recv.at[q, 2], ss.at[q, 2], sr.at[q, 2], z_peer(1))
        send(buf.at[block(-3), r], recv.at[q, 3], ss.at[q, 3], sr.at[q, 3], z_peer(-1))
        send(buf.at[block(4), low], half.at[q, 0], ss.at[q, 6], sr.at[q, 6], z_peer(2))
        send(buf.at[block(4), high], half.at[q, 1], ss.at[q, 7], sr.at[q, 7], z_peer(-2))
        send(buf.at[block(1), r], recv.at[q, 0], ss.at[q, 0], sr.at[q, 0], z_peer(1))
        send(buf.at[block(-1), r], recv.at[q, 1], ss.at[q, 1], sr.at[q, 1], z_peer(-1))

    def z_second(q, buf, recv, half, ss, sr):
        r = rows_of(q)
        for n, way in ((0, 2), (1, -2)):
            arrived(recv.at[q, 2 + n], ss.at[q, 2 + n], sr.at[q, 2 + n])
            arrived(half.at[q, n], ss.at[q, 6 + n], sr.at[q, 6 + n])
            total = buf[block(way), r].astype(F32) + recv[q, 2 + n].astype(F32)
            extra = half[q, n].astype(F32)
            zeros = jnp.zeros_like(extra)
            total = total + jnp.concatenate([extra, zeros] if n == 0 else [zeros, extra], axis=0)
            buf[block(way), r] = total.astype(BF16)
            send(buf.at[block(way), r], recv.at[q, 4 + n], ss.at[q, 4 + n], sr.at[q, 4 + n], z_peer(way))

    def z_total(q, own, recv, ss, sr):
        total = own
        for n in (0, 1, 4, 5):
            arrived(recv.at[q, n], ss.at[q, n], sr.at[q, n])
            total = total + recv[q, n].astype(F32)
        return total

    def b1(q):
        send(a.at[:, 1 - c, rows_of(q)], ar.at[q], b_s.at[q], b_r.at[q], sibling)

    def b2(q):
        arrived(ar.at[q], b_s.at[q], b_r.at[q])
        both = a[:, c, rows_of(q)].astype(F32) + ar[q].astype(F32)
        ah[:, rows_of(q)] = both.astype(BF16)
        z_first(q, ah, az, azh, bz_s, bz_r)

    def b3(q):
        z_second(q, ah, az, azh, bz_s, bz_r)

    def c1(q):
        if q == 0:
            loads[5].wait()
        r = rows_of(q)
        own = a[z, c, r].astype(F32) + ar[q, z].astype(F32)
        stream = res_v[r].astype(F32) + z_total(q, own, az, bz_s, bz_r)
        st[z, r] = stream.astype(BF16)
        mine = st.at[z, r]
        for n, way in ((2, 2), (3, -2), (0, 1), (1, -1)):
            send(mine, mine, cz_s.at[q, n], cz_r.at[q, n], z_peer(way))

    def c2(q):
        r = rows_of(q)
        low, high = pl.ds(R * q, R // 2), pl.ds(R * q + R // 2, R // 2)
        mine = st.at[z, r]
        for n, way, part in ((0, 1, low), (1, -1, high)):
            arrived(mine, cz_s.at[q, 2 + n], cz_r.at[q, 2 + n])
            far = block(-2 * way)
            send(st.at[far, r], st.at[far, r], cz_s.at[q, 4 + n], cz_r.at[q, 4 + n], z_peer(way))
            send(st.at[far, part], st.at[far, part], cz_s.at[q, 6 + n], cz_r.at[q, 6 + n], z_peer(2 * way))

    def cube(order, step, flip):
        at = [slice(None)] * 4
        for n in range(step):
            at[order[n]] = bits[order[n]]
        at[order[step]] = 1 - bits[order[step]] if flip else bits[order[step]]
        return tuple(at)

    def d_lanes(q, i):
        return (slice(None), pl.ds(0, FF + 128 if i == q else FF))

    def d_send(q, i, step):
        order = ORDERS[i]
        where = (q, i) + cube(order, step, True) + d_lanes(q, i)
        if step > 0:
            total = p[where].astype(F32)
            for n in range(step):
                total = total + rs[n][where].astype(F32)
            p[where] = total.astype(BF16)
        send(p.at[where], rs[step].at[where], d_s.at[q, i, step], d_r.at[q, i, step], near[order[step]])

    def d_arrived(q, i, step):
        where = (q, i) + cube(ORDERS[i], step, False) + d_lanes(q, i)
        arrived(rs[step].at[where], d_s.at[q, i, step], d_r.at[q, i, step])

    def d1(q):
        if q == 0:
            arrived(gu_v.at[0:2], w_s.at[0], w_r.at[0])
        r = rows_of(q)
        mine = st.at[z, r]
        for n in (0, 1, 4, 5):
            arrived(mine, cz_s.at[q, n], cz_r.at[q, n])
        for n in (6, 7):
            arrived(st.at[z, pl.ds(R * q, R // 2)], cz_s.at[q, n], cz_r.at[q, n])
        wide = st[:, r].reshape(8 * R, W).astype(F32)
        scaled = (wide * gain[...].astype(F32).reshape(1, W)).astype(BF16)
        for i in range(4):
            part = dot(scaled, gu_v[i]).astype(BF16)
            p[q, i, :, :, :, :, :, 0:FF] = part.reshape(2, 2, 2, 2, RD, FF)
            if i == q:
                squares = jnp.sum(wide * wide, axis=1, keepdims=True)
                squares = jnp.broadcast_to(squares, (8 * R, 128)).astype(BF16)
                p[q, i, :, :, :, :, :, FF:FF + 128] = squares.reshape(2, 2, 2, 2, RD, 128)
            d_send(q, i, 0)

    def d_next(q, step):
        for i in range(4):
            d_arrived(q, i, step - 1)
            d_send(q, i, step)

    def e_ref(q, i, step):
        order = ORDERS[i]
        at = [slice(None)] * 4
        for n in range(4 - step):
            at[order[n]] = bits[order[n]]
        return tuple(at)

    def e_send(q, i, step):
        where = (q,) + e_ref(q, i, step)
        dim = ORDERS[i][3 - step]
        send(hs[i].at[where], hs[i].at[where], e_s.at[q, i, step], e_r.at[q, i, step], near[dim])

    def e_arrived(q, i, step):
        at = list(e_ref(q, i, step))
        dim = ORDERS[i][3 - step]
        at[dim] = 1 - bits[dim]
        arrived(hs[i].at[(q,) + tuple(at)], e_s.at[q, i, step], e_r.at[q, i, step])

    def d5(q):
        sums = []
        for i in range(4):
            d_arrived(q, i, 3)
            at = (q, i) + tuple(bits) + d_lanes(q, i)
            total = p[at].astype(F32)
            for n in range(4):
                total = total + rs[n][at].astype(F32)
            sums.append(total)
        inverse = lax.rsqrt(sums[q][:, FF:FF + 128] / D + EPS)
        for i in range(4):
            for n in range(*E_TILES[i]):
                lanes = slice(128 * (n % 7), 128 * (n % 7) + 128)
                gate = sums[2 * (n // 7)][:, lanes] * inverse
                up = sums[2 * (n // 7) + 1][:, lanes] * inverse
                hidden = gate / (1.0 + jnp.exp(-gate)) * up
                at = 128 * (n - E_TILES[i][0])
                hs[i][(q,) + tuple(bits) + (slice(None), slice(at, at + 128))] = hidden.astype(BF16)
            e_send(q, i, 0)

    def e_next(q, step):
        for i in range(4):
            e_arrived(q, i, step - 1)
            e_send(q, i, step)

    def f1(q):
        if q == 0:
            arrived(dw_v.at[1], w_s.at[1], w_r.at[1])
        down = dw_v[...].reshape(2 * FF, W)
        total = None
        for i in range(4):
            e_arrived(q, i, 3)
            lo, hi = E_TILES[i]
            part = dot(hs[i][q].reshape(8 * R, 128 * (hi - lo)), down[128 * lo:128 * hi])
            total = part if total is None else total + part
        f[:, rows_of(q)] = total.astype(BF16).reshape(8, R, W)
        z_first(q, f, fz, fzh, fz_s, fz_r)

    def f2(q):
        z_second(q, f, fz, fzh, fz_s, fz_r)

    def f3(q):
        r = rows_of(q)
        total = z_total(q, f[z, r].astype(F32), fz, fz_s, fz_r)
        out[r] = (st[z, r].astype(F32) + total).astype(BF16)

    stages = [b1, b2, b3, c1, c2, d1]
    stages += [functools.partial(d_next, step=s) for s in (1, 2, 3)] + [d5]
    stages += [functools.partial(e_next, step=s) for s in (1, 2, 3)] + [f1, f2, f3]
    for stage in stages:
        for q in range(NQ):
            stage(q)
    for cp in sends:
        cp.wait_send()


def local(head_out, residual, class_ids, head_mask, out_weight, norm_gain, gate_up, down_weight):
    hbm = pl.BlockSpec(memory_space=pl.ANY)
    vmem = pl.BlockSpec(memory_space=pltpu.VMEM)
    smem = pl.BlockSpec(memory_space=pltpu.SMEM)
    dma = pltpu.SemaphoreType.DMA
    cube = (NQ, 4, 2, 2, 2, 2, RD, FF + 128)
    return pl.pallas_call(
        kernel,
        out_shape=jax.ShapeDtypeStruct((64, W), BF16),
        in_specs=[hbm, hbm, vmem, smem, hbm, vmem, hbm, hbm],
        out_specs=vmem,
        scratch_shapes=[
            pltpu.VMEM((W, W), BF16),
            pltpu.VMEM((W, 2, FF), BF16),
            pltpu.VMEM((4, W, FF), BF16),
            pltpu.VMEM((2, FF, W), BF16),
            pltpu.VMEM((64, W), BF16),
            pltpu.VMEM((2, 4, 4, 64, 256), BF16),
            pltpu.VMEM((CLASSES, TOKENS), BF16),
            pltpu.VMEM((TOKENS, CLASSES), BF16),
            pltpu.VMEM((8, 2, 64, W), BF16),
            pltpu.VMEM((NQ, 8, R, W), BF16),
            pltpu.VMEM((NQ, 6, R, W), BF16),
            pltpu.VMEM((NQ, 2, R // 2, W), BF16),
            pltpu.VMEM((8, 64, W), BF16),
            pltpu.VMEM((8, 64, W), BF16),
            *[pltpu.VMEM(cube, BF16) for _ in range(5)],
            *[pltpu.VMEM((NQ, 2, 2, 2, 2, RD, 128 * (hi - lo)), BF16) for lo, hi in E_TILES],
            pltpu.VMEM((8, 64, W), BF16),
            pltpu.VMEM((NQ, 6, R, W), BF16),
            pltpu.VMEM((NQ, 2, R // 2, W), BF16),
            dma((6,)),
            dma((2,)), dma((2,)),
            dma((2, 4)), dma((2, 4)),
            dma((2, 4, 4)), dma((2, 4, 4)),
            dma((NQ,)), dma((NQ,)),
            dma((NQ, 8)), dma((NQ, 8)),
            dma((NQ, 8)), dma((NQ, 8)),
            dma((NQ, 4, 4)), dma((NQ, 4, 4)),
            dma((NQ, 4, 4)), dma((NQ, 4, 4)),
            dma((NQ, 8)), dma((NQ, 8)),
        ],
        compiler_params=pltpu.CompilerParams(
            collective_id=0, has_side_effects=True, vmem_limit_bytes=56 << 20
        ),
        name="layer",
    )(head_out, residual, class_ids.reshape(1, TOKENS), head_mask, out_weight, norm_gain,
      gate_up, down_weight)


def solution(mesh):
    in_specs = (
        P("dp", "tensor"),
        P("tensor", "dp"),
        P(),
        P("tensor"),
        P("tensor", "dp"),
        P("dp"),
        P("dp", None, "tensor"),
        P("tensor", "dp"),
    )
    return jax.shard_map(local, mesh=mesh, in_specs=in_specs, out_specs=P("tensor", "dp"), check_vma=False)
```

```python
import functools

import jax
import jax.numpy as jnp
from jax import lax
from jax.experimental import pallas as pl
from jax.experimental.pallas import tpu as pltpu
from jax.sharding import PartitionSpec as P

MESH = pl.DeviceIdType.MESH
BF16 = jnp.bfloat16
F32 = jnp.float32
D = 8192
HEAD_DIM = 128
CLASSES = 256
EPS = 1e-05
TOKENS = 1024
W = 512
FF = 896
NQ = 2
R = 64 // NQ
RD = R // 2
ORDERS = ((3, 2, 1, 0), (2, 3, 0, 1), (1, 0, 3, 2), (0, 1, 2, 3))
E_TILES = ((0, 4), (4, 8), (8, 11), (11, 14))


def dot(a, b):
    return jnp.dot(a, b, preferred_element_type=F32)


def kernel(ho, res, ids, mask, ow, gain, gu, dw, out,
           ow_v, gu_in, gu_v, dw_v, res_v, g, oh, oht, mean, a, ar, af, az, azh, ah, st, p, r1, r2, r3, h0, h1, h2, h3, f, fz, fzh,
           load_sem, w_s, w_r, x_s, x_r, a_s, a_r, b_s, b_r, bz_s, bz_r, cz_s, cz_r, d_s, d_r, e_s, e_r, fz_s, fz_r):
    dp = lax.axis_index("dp")
    tn = lax.axis_index("tensor")
    y, x = dp // 4, dp % 4
    z, c = tn // 2, tn % 2
    rs = (r1, r2)
    hs = (h0, h1, h2, h3)
    bits = (y // 2, (y + y // 2) % 2, x // 2, (x + x // 2) % 2)
    near = (
        ((3 - y) * 4 + x, tn),
        ((y + 1 - 2 * (y % 2)) * 4 + x, tn),
        (y * 4 + 3 - x, tn),
        (y * 4 + x + 1 - 2 * (x % 2), tn),
    )
    sibling = (dp, z * 2 + 1 - c)

    def x_peer(k):
        return (y * 4 + (x + k) % 4, tn)

    def y_peer(k):
        return (((y + k) % 4) * 4 + x, tn)

    def z_peer(k):
        return (dp, ((z + k + 8) % 8) * 2 + c)

    def block(k):
        return (z + k + 8) % 8

    sends = []

    def send(src, dst, ssem, rsem, to):
        cp = pltpu.make_async_remote_copy(src_ref=src, dst_ref=dst, send_sem=ssem, recv_sem=rsem,
                                          device_id=to, device_id_type=MESH)
        cp.start()
        sends.append(cp)

    def arrived(ref, ssem, rsem):
        pltpu.make_async_remote_copy(src_ref=ref, dst_ref=ref, send_sem=ssem, recv_sem=rsem,
                                     device_id=sibling, device_id_type=MESH).wait_recv()

    loads = [
        pltpu.make_async_copy(ho.at[:, 0:256], g.at[0, dp // 2, dp % 2], load_sem.at[0]),
        pltpu.make_async_copy(ho.at[:, 256:512], g.at[1, dp // 2, dp % 2], load_sem.at[1]),
        pltpu.make_async_copy(gu, gu_in, load_sem.at[2]),
        pltpu.make_async_copy(dw, dw_v.at[0], load_sem.at[3]),
        pltpu.make_async_copy(ow, ow_v, load_sem.at[4]),
        pltpu.make_async_copy(res, res_v, load_sem.at[5]),
    ]
    for cp in loads:
        cp.start()

    barrier = pltpu.get_barrier_semaphore()
    peers = [x_peer(k) for k in (1, 2, 3)] + [y_peer(k) for k in (1, 2, 3)] + [z_peer(k) for k in (1, -1, 2, -2)] + [sibling]
    for to in peers:
        pl.semaphore_signal(barrier, inc=1, device_id=to, device_id_type=MESH)

    loads[0].wait()
    loads[1].wait()
    pl.semaphore_wait(barrier, len(peers))

    first = ((x_peer, y_peer), (y_peer, x_peer))
    mine = [g.at[h, dp // 2, dp % 2] for h in (0, 1)]
    for k in (1, 3, 2):
        for h in (0, 1):
            send(mine[h], mine[h], x_s.at[h, k], x_r.at[h, k], first[h][0](k))
    for k in (1, 3, 2):
        for h in (0, 1):
            send(mine[h], mine[h], a_s.at[h, 0, k], a_r.at[h, 0, k], first[h][1](k))
    loads[3].wait()
    send(dw_v.at[0], dw_v.at[1], w_s.at[1], w_r.at[1], sibling)
    same = lax.broadcasted_iota(jnp.int32, (CLASSES, TOKENS), 0) == ids[...]
    onehot = same.astype(F32)
    counts = jnp.sum(onehot, axis=1, keepdims=True)
    oh[...] = onehot.astype(BF16)
    for j in (1, 3, 2):
        for h in (0, 1):
            source = y * 4 + (x - j + 4) % 4 if h == 0 else (y - j + 4) % 4 * 4 + x
            got = g.at[h, source // 2, source % 2]
            arrived(got, x_s.at[h, j], x_r.at[h, j])
            for k in (1, 3, 2):
                send(got, got, a_s.at[h, j, k], a_r.at[h, j, k], first[h][1](k))
    oht[...] = onehot.T.astype(BF16).reshape(8, 2, 64, CLASSES)
    loads[2].wait()
    gu_v[0] = gu_in[:, 0, :]
    gu_v[1] = gu_in[:, 1, :]
    send(gu_v.at[0:2], gu_v.at[2:4], w_s.at[0], w_r.at[0], sibling)
    for j in range(4):
        for k in (1, 2, 3):
            for h in (0, 1):
                arrived(mine[h], a_s.at[h, j, k], a_r.at[h, j, k])

    for h in (0, 1):
        totals = dot(oh[...], g[h].reshape(TOKENS, 256))
        mean[h] = (totals / jnp.maximum(counts, 1.0)).astype(BF16)
    lane_head = lax.broadcasted_iota(jnp.int32, (1, 256), 1) // HEAD_DIM
    ablate = [jnp.where(lane_head == 0, mask[2 * h], mask[2 * h + 1]) == 1 for h in (0, 1)]
    loads[4].wait()

    def share(q, core):
        rows = oht[:, core, rows_of(q)].reshape(8 * R, CLASSES)
        total = None
        for h in (0, 1):
            looked = dot(rows, mean[h])
            kept = g[h, :, core, rows_of(q)].reshape(8 * R, 256).astype(F32)
            patched = jnp.where(ablate[h], looked, kept).astype(BF16)
            part = dot(patched, ow_v[256 * h:256 * h + 256])
            total = part if total is None else total + part
        return total.reshape(8, R, W)

    def rows_of(q):
        return pl.ds(R * q, R)

    def z_first(q, buf, recv, half, ss, sr):
        r = rows_of(q)
        low, high = pl.ds(R * q, R // 2), pl.ds(R * q + R // 2, R // 2)
        send(buf.at[block(3), r], recv.at[q, 2], ss.at[q, 2], sr.at[q, 2], z_peer(1))
        send(buf.at[block(-3), r], recv.at[q, 3], ss.at[q, 3], sr.at[q, 3], z_peer(-1))
        send(buf.at[block(4), low], half.at[q, 0], ss.at[q, 6], sr.at[q, 6], z_peer(2))
        send(buf.at[block(4), high], half.at[q, 1], ss.at[q, 7], sr.at[q, 7], z_peer(-2))
        send(buf.at[block(1), r], recv.at[q, 0], ss.at[q, 0], sr.at[q, 0], z_peer(1))
        send(buf.at[block(-1), r], recv.at[q, 1], ss.at[q, 1], sr.at[q, 1], z_peer(-1))

    def z_second(q, buf, recv, half, ss, sr):
        r = rows_of(q)
        for n, way in ((0, 2), (1, -2)):
            arrived(recv.at[q, 2 + n], ss.at[q, 2 + n], sr.at[q, 2 + n])
            arrived(half.at[q, n], ss.at[q, 6 + n], sr.at[q, 6 + n])
            total = buf[block(way), r].astype(F32) + recv[q, 2 + n].astype(F32)
            extra = half[q, n].astype(F32)
            zeros = jnp.zeros_like(extra)
            total = total + jnp.concatenate([extra, zeros] if n == 0 else [zeros, extra], axis=0)
            buf[block(way), r] = total.astype(BF16)
            send(buf.at[block(way), r], recv.at[q, 4 + n], ss.at[q, 4 + n], sr.at[q, 4 + n], z_peer(way))

    def z_total(q, own, recv, ss, sr):
        total = own
        for n in (0, 1, 4, 5):
            arrived(recv.at[q, n], ss.at[q, n], sr.at[q, n])
            total = total + recv[q, n].astype(F32)
        return total

    def b1(q):
        a[q] = share(q, 1 - c).astype(BF16)
        send(a.at[q], ar.at[q], b_s.at[q], b_r.at[q], sibling)

    def b2(q):
        both = share(q, c)
        arrived(ar.at[q], b_s.at[q], b_r.at[q])
        both = both + ar[q].astype(F32)
        af[q] = both
        ah[:, rows_of(q)] = both.astype(BF16)
        z_first(q, ah, az, azh, bz_s, bz_r)

    def b3(q):
        z_second(q, ah, az, azh, bz_s, bz_r)

    def c1(q):
        if q == 0:
            loads[5].wait()
        r = rows_of(q)
        stream = res_v[r].astype(F32) + z_total(q, af[q, z], az, bz_s, bz_r)
        st[z, r] = stream.astype(BF16)
        mine = st.at[z, r]
        for n, way in ((2, 2), (3, -2), (0, 1), (1, -1)):
            send(mine, mine, cz_s.at[q, n], cz_r.at[q, n], z_peer(way))

    def c2(q):
        r = rows_of(q)
        low, high = pl.ds(R * q, R // 2), pl.ds(R * q + R // 2, R // 2)
        mine = st.at[z, r]
        for n, way, part in ((0, 1, low), (1, -1, high)):
            arrived(mine, cz_s.at[q, 2 + n], cz_r.at[q, 2 + n])
            far = block(-2 * way)
            send(st.at[far, r], st.at[far, r], cz_s.at[q, 4 + n], cz_r.at[q, 4 + n], z_peer(way))
            send(st.at[far, part], st.at[far, part], cz_s.at[q, 6 + n], cz_r.at[q, 6 + n], z_peer(2 * way))

    def cube(order, step, flip):
        at = [slice(None)] * 4
        for n in range(step):
            at[order[n]] = bits[order[n]]
        at[order[step]] = 1 - bits[order[step]] if flip else bits[order[step]]
        return tuple(at)

    def d_lanes(q, i):
        return (slice(None), pl.ds(0, FF + 128 if i == q else FF))

    def d_send(q, i, step):
        order = ORDERS[i]
        where = (q, i) + cube(order, step, True) + d_lanes(q, i)
        if step > 0:
            total = p[where].astype(F32)
            for n in range(step):
                total = total + rs[n][where].astype(F32)
            p[where] = total.astype(BF16)
        send(p.at[where], rs[step].at[where], d_s.at[q, i, step], d_r.at[q, i, step], near[order[step]])

    def d_arrived(q, i, step):
        where = (q, i) + cube(ORDERS[i], step, False) + d_lanes(q, i)
        arrived(rs[step].at[where], d_s.at[q, i, step], d_r.at[q, i, step])

    def d1(q):
        if q == 0:
            arrived(gu_v.at[0:2], w_s.at[0], w_r.at[0])
        r = rows_of(q)
        mine = st.at[z, r]
        for n in (0, 1, 4, 5):
            arrived(mine, cz_s.at[q, n], cz_r.at[q, n])
        for n in (6, 7):
            arrived(st.at[z, pl.ds(R * q, R // 2)], cz_s.at[q, n], cz_r.at[q, n])
        wide = st[:, r].reshape(8 * R, W).astype(F32)
        scaled = (wide * gain[...].astype(F32).reshape(1, W)).astype(BF16)
        for i in range(4):
            part = dot(scaled, gu_v[i]).astype(BF16)
            p[q, i, :, :, :, :, :, 0:FF] = part.reshape(2, 2, 2, 2, RD, FF)
            if i == q:
                squares = jnp.sum(wide * wide, axis=1, keepdims=True)
                squares = jnp.broadcast_to(squares, (8 * R, 128)).astype(BF16)
                p[q, i, :, :, :, :, :, FF:FF + 128] = squares.reshape(2, 2, 2, 2, RD, 128)
            d_send(q, i, 0)

    def d_next(q, step):
        for i in range(4):
            d_arrived(q, i, step - 1)
            d_send(q, i, step)

    def last_axis(i):
        return (x_peer, x, (2, 3)) if ORDERS[i][0] < 2 else (y_peer, y, (0, 1))

    def bits_at(i, k):
        _, at, dims = last_axis(i)
        there = (at + k) % 4
        full = list(bits)
        full[dims[0]], full[dims[1]] = there // 2, (there + there // 2) % 2
        return tuple(full)

    def d3(q):
        for i in range(4):
            d_arrived(q, i, 1)
            for k in (2, 1, 3):
                where = (q, i) + bits_at(i, k) + d_lanes(q, i)
                total = p[where].astype(F32) + r1[where].astype(F32) + r2[where].astype(F32)
                p[where] = total.astype(BF16)
                send(p.at[where], r3.at[(q, i, k) + d_lanes(q, i)], d_s.at[q, i, 1 + k], d_r.at[q, i, 1 + k], last_axis(i)[0](k))

    def d4(q):
        sums = []
        for i in range(4):
            at = (q, i) + tuple(bits) + d_lanes(q, i)
            total = p[at].astype(F32) + r1[at].astype(F32) + r2[at].astype(F32)
            for k in (1, 3, 2):
                at = (q, i, k) + d_lanes(q, i)
                arrived(r3.at[at], d_s.at[q, i, 1 + k], d_r.at[q, i, 1 + k])
                total = total + r3[at].astype(F32)
            sums.append(total)
        inverse = lax.rsqrt(sums[q][:, FF:FF + 128] / D + EPS)
        for i in range(4):
            for n in range(*E_TILES[i]):
                lanes = slice(128 * (n % 7), 128 * (n % 7) + 128)
                gate = sums[2 * (n // 7)][:, lanes] * inverse
                up = sums[2 * (n // 7) + 1][:, lanes] * inverse
                hidden = gate / (1.0 + jnp.exp(-gate)) * up
                at = 128 * (n - E_TILES[i][0])
                hs[i][(q,) + tuple(bits) + (slice(None), slice(at, at + 128))] = hidden.astype(BF16)
            ref = hs[i].at[(q,) + tuple(bits)]
            for k in (2, 1, 3):
                send(ref, ref, e_s.at[q, i, k - 1], e_r.at[q, i, k - 1], last_axis(i)[0](k))

    def e_ref(q, i, step):
        order = ORDERS[i]
        at = [slice(None)] * 4
        for n in range(2 - step):
            at[order[n]] = bits[order[n]]
        return at

    def e_send(q, i, step):
        where = (q,) + tuple(e_ref(q, i, step))
        send(hs[i].at[where], hs[i].at[where], e_s.at[q, i, 3 + step], e_r.at[q, i, 3 + step], near[ORDERS[i][1 - step]])

    def e_arrived(q, i, step):
        at = e_ref(q, i, step)
        dim = ORDERS[i][1 - step]
        at[dim] = 1 - bits[dim]
        arrived(hs[i].at[(q,) + tuple(at)], e_s.at[q, i, 3 + step], e_r.at[q, i, 3 + step])

    def e2(q):
        for i in range(4):
            ref = hs[i].at[(q,) + tuple(bits)]
            for k in (1, 3, 2):
                arrived(ref, e_s.at[q, i, k - 1], e_r.at[q, i, k - 1])
            e_send(q, i, 0)

    def e3(q):
        for i in range(4):
            e_arrived(q, i, 0)
            e_send(q, i, 1)

    def f1(q):
        if q == 0:
            arrived(dw_v.at[1], w_s.at[1], w_r.at[1])
        down = dw_v[...].reshape(2 * FF, W)
        total = None
        for i in range(4):
            e_arrived(q, i, 1)
            lo, hi = E_TILES[i]
            part = dot(hs[i][q].reshape(8 * R, 128 * (hi - lo)), down[128 * lo:128 * hi])
            total = part if total is None else total + part
        f[:, rows_of(q)] = total.astype(BF16).reshape(8, R, W)
        z_first(q, f, fz, fzh, fz_s, fz_r)

    def f2(q):
        z_second(q, f, fz, fzh, fz_s, fz_r)

    def f3(q):
        r = rows_of(q)
        total = z_total(q, f[z, r].astype(F32), fz, fz_s, fz_r)
        out[r] = (st[z, r].astype(F32) + total).astype(BF16)

    d2 = functools.partial(d_next, step=1)
    for stage in (b1, b2, b3, c1, c2, d1, d2, d3, d4, e2, e3, f1, f2, f3):
        for q in range(NQ):
            stage(q)
    for cp in sends:
        cp.wait_send()


def local(head_out, residual, class_ids, head_mask, out_weight, norm_gain, gate_up, down_weight):
    hbm = pl.BlockSpec(memory_space=pl.ANY)
    vmem = pl.BlockSpec(memory_space=pltpu.VMEM)
    smem = pl.BlockSpec(memory_space=pltpu.SMEM)
    dma = pltpu.SemaphoreType.DMA
    cube = (NQ, 4, 2, 2, 2, 2, RD, FF + 128)
    return pl.pallas_call(
        kernel,
        out_shape=jax.ShapeDtypeStruct((64, W), BF16),
        in_specs=[hbm, hbm, vmem, smem, hbm, vmem, hbm, hbm],
        out_specs=vmem,
        scratch_shapes=[
            pltpu.VMEM((W, W), BF16),
            pltpu.VMEM((W, 2, FF), BF16),
            pltpu.VMEM((4, W, FF), BF16),
            pltpu.VMEM((2, FF, W), BF16),
            pltpu.VMEM((64, W), BF16),
            pltpu.VMEM((2, 8, 2, 64, 256), BF16),
            pltpu.VMEM((CLASSES, TOKENS), BF16),
            pltpu.VMEM((8, 2, 64, CLASSES), BF16),
            pltpu.VMEM((2, CLASSES, 256), BF16),
            pltpu.VMEM((NQ, 8, R, W), BF16),
            pltpu.VMEM((NQ, 8, R, W), BF16),
            pltpu.VMEM((NQ, 8, R, W), F32),
            pltpu.VMEM((NQ, 6, R, W), BF16),
            pltpu.VMEM((NQ, 2, R // 2, W), BF16),
            pltpu.VMEM((8, 64, W), BF16),
            pltpu.VMEM((8, 64, W), BF16),
            *[pltpu.VMEM(cube, BF16) for _ in range(3)],
            pltpu.VMEM((NQ, 4, 4, RD, FF + 128), BF16),
            *[pltpu.VMEM((NQ, 2, 2, 2, 2, RD, 128 * (hi - lo)), BF16) for lo, hi in E_TILES],
            pltpu.VMEM((8, 64, W), BF16),
            pltpu.VMEM((NQ, 6, R, W), BF16),
            pltpu.VMEM((NQ, 2, R // 2, W), BF16),
            dma((6,)),
            dma((2,)), dma((2,)),
            dma((2, 4)), dma((2, 4)),
            dma((2, 4, 4)), dma((2, 4, 4)),
            dma((NQ,)), dma((NQ,)),
            dma((NQ, 8)), dma((NQ, 8)),
            dma((NQ, 8)), dma((NQ, 8)),
            dma((NQ, 4, 5)), dma((NQ, 4, 5)),
            dma((NQ, 4, 5)), dma((NQ, 4, 5)),
            dma((NQ, 8)), dma((NQ, 8)),
        ],
        compiler_params=pltpu.CompilerParams(
            collective_id=0, has_side_effects=True, vmem_limit_bytes=56 << 20
        ),
        name="layer",
    )(head_out, residual, class_ids.reshape(1, TOKENS), head_mask, out_weight, norm_gain,
      gate_up, down_weight)


def solution(mesh):
    in_specs = (
        P("dp", "tensor"),
        P("tensor", "dp"),
        P(),
        P("tensor"),
        P("tensor", "dp"),
        P("dp"),
        P("dp", None, "tensor"),
        P("tensor", "dp"),
    )
    return jax.shard_map(local, mesh=mesh, in_specs=in_specs, out_specs=P("tensor", "dp"), check_vma=False)
```

```python
import jax
import jax.numpy as jnp
from jax import lax
from jax.experimental import pallas as pl
from jax.experimental.pallas import tpu as pltpu
from jax.sharding import PartitionSpec as P

MESH = pl.DeviceIdType.MESH
BF16 = jnp.bfloat16
F32 = jnp.float32
D = 8192
HEAD_DIM = 128
CLASSES = 256
EPS = 1e-05
TOKENS = 1024
W = 512
FF = 896
NQ = 2
R = 64 // NQ
RD = R // 2
ORDERS = ((3, 2, 1, 0), (2, 3, 0, 1), (1, 0, 3, 2), (0, 1, 2, 3))
D_TILES = (((0, 4), (4, 8), (8, 11), (11, 14)), ((0, 3), (3, 6), (6, 10), (10, 14)))
E_TILES = (((0, 2), (2, 4), (4, 6), (6, 7)), ((0, 1), (1, 3), (3, 5), (5, 7)))


def dot(a, b):
    return jnp.dot(a, b, preferred_element_type=F32)


def kernel(ho, res, ids, mask, ow, gain, gu, dw, out,
           ow_v, gu_in, gu_v, dw_v, res_v, g, oh, oht, mean, a, ar, af, az, azh, ah, st, sc, inv, sq, sqx, sqy, p, r1, r2, r3, h0, h1, h2, h3, f, fz, fzh,
           load_sem, w_s, w_r, x_s, x_r, a_s, a_r, b_s, b_r, bz_s, bz_r, cz_s, cz_r, d_s, d_r, q_s, q_r, e_s, e_r, fz_s, fz_r):
    dp = lax.axis_index("dp")
    tn = lax.axis_index("tensor")
    y, x = dp // 4, dp % 4
    z, c = tn // 2, tn % 2
    rs = (r1, r2)
    hs = (h0, h1, h2, h3)
    bits = (y // 2, (y + y // 2) % 2, x // 2, (x + x // 2) % 2)
    near = (
        ((3 - y) * 4 + x, tn),
        ((y + 1 - 2 * (y % 2)) * 4 + x, tn),
        (y * 4 + 3 - x, tn),
        (y * 4 + x + 1 - 2 * (x % 2), tn),
    )
    sibling = (dp, z * 2 + 1 - c)

    def x_peer(k):
        return (y * 4 + (x + k) % 4, tn)

    def y_peer(k):
        return (((y + k) % 4) * 4 + x, tn)

    def z_peer(k):
        return (dp, ((z + k + 8) % 8) * 2 + c)

    def block(k):
        return (z + k + 8) % 8

    sends = []

    def send(src, dst, ssem, rsem, to):
        cp = pltpu.make_async_remote_copy(src_ref=src, dst_ref=dst, send_sem=ssem, recv_sem=rsem,
                                          device_id=to, device_id_type=MESH)
        cp.start()
        sends.append(cp)

    def arrived(ref, ssem, rsem):
        while len(sends) > 48:
            sends.pop(0).wait_send()
        pltpu.make_async_remote_copy(src_ref=ref, dst_ref=ref, send_sem=ssem, recv_sem=rsem,
                                     device_id=sibling, device_id_type=MESH).wait_recv()

    loads = [
        pltpu.make_async_copy(ho.at[:, 0:256], g.at[0, dp // 2, dp % 2], load_sem.at[0]),
        pltpu.make_async_copy(ho.at[:, 256:512], g.at[1, dp // 2, dp % 2], load_sem.at[1]),
        pltpu.make_async_copy(gu, gu_in, load_sem.at[2]),
        pltpu.make_async_copy(dw, dw_v.at[0], load_sem.at[3]),
        pltpu.make_async_copy(ow, ow_v, load_sem.at[4]),
        pltpu.make_async_copy(res, res_v, load_sem.at[5]),
    ]
    for cp in loads:
        cp.start()

    barrier = pltpu.get_barrier_semaphore()
    peers = [x_peer(k) for k in (1, 2, 3)] + [y_peer(k) for k in (1, 2, 3)] + [z_peer(k) for k in (1, -1, 2, -2)] + [sibling]
    for to in peers:
        pl.semaphore_signal(barrier, inc=1, device_id=to, device_id_type=MESH)

    pl.semaphore_wait(barrier, len(peers))

    first = ((x_peer, y_peer), (y_peer, x_peer))
    mine = [ho.at[:, 256 * h:256 * h + 256] for h in (0, 1)]
    slot = [g.at[h, dp // 2, dp % 2] for h in (0, 1)]
    for k in (1, 3, 2):
        for h in (0, 1):
            send(mine[h], slot[h], x_s.at[h, k], x_r.at[h, k], first[h][0](k))
    for k in (1, 3, 2):
        for h in (0, 1):
            send(mine[h], slot[h], a_s.at[h, 0, k], a_r.at[h, 0, k], first[h][1](k))
    loads[3].wait()
    send(dw_v.at[0], dw_v.at[1], w_s.at[1], w_r.at[1], sibling)
    same = lax.broadcasted_iota(jnp.int32, (CLASSES, TOKENS), 0) == ids[...]
    onehot = same.astype(F32)
    counts = jnp.sum(onehot, axis=1, keepdims=True)
    oh[...] = onehot.astype(BF16)
    for j in (1, 3, 2):
        for h in (0, 1):
            source = y * 4 + (x - j + 4) % 4 if h == 0 else (y - j + 4) % 4 * 4 + x
            got = g.at[h, source // 2, source % 2]
            arrived(got, x_s.at[h, j], x_r.at[h, j])
            for k in (1, 3, 2):
                send(got, got, a_s.at[h, j, k], a_r.at[h, j, k], first[h][1](k))
    oht[...] = onehot.T.astype(BF16).reshape(8, 2, 64, CLASSES)
    for j in range(4):
        for k in (1, 2, 3):
            for h in (0, 1):
                arrived(slot[h], a_s.at[h, j, k], a_r.at[h, j, k])

    loads[0].wait()
    loads[1].wait()

    for h in (0, 1):
        totals = dot(oh[...], g[h].reshape(TOKENS, 256))
        mean[h] = (totals / jnp.maximum(counts, 1.0)).astype(BF16)
    lane_head = lax.broadcasted_iota(jnp.int32, (1, 256), 1) // HEAD_DIM
    ablate = [jnp.where(lane_head == 0, mask[2 * h], mask[2 * h + 1]) == 1 for h in (0, 1)]
    loads[4].wait()

    def share(q, core):
        rows = oht[:, core, rows_of(q)].reshape(8 * R, CLASSES)
        total = None
        for h in (0, 1):
            looked = dot(rows, mean[h])
            kept = g[h, :, core, rows_of(q)].reshape(8 * R, 256).astype(F32)
            patched = jnp.where(ablate[h], looked, kept).astype(BF16)
            part = dot(patched, ow_v[256 * h:256 * h + 256])
            total = part if total is None else total + part
        return total.reshape(8, R, W)

    def rows_of(q):
        return pl.ds(R * q, R)

    def z_first(q, buf, recv, half, ss, sr):
        r = rows_of(q)
        low, high = pl.ds(R * q, R // 2), pl.ds(R * q + R // 2, R // 2)
        send(buf.at[block(3), r], recv.at[q, 2], ss.at[q, 2], sr.at[q, 2], z_peer(1))
        send(buf.at[block(-3), r], recv.at[q, 3], ss.at[q, 3], sr.at[q, 3], z_peer(-1))
        send(buf.at[block(4), low], half.at[q, 0], ss.at[q, 6], sr.at[q, 6], z_peer(2))
        send(buf.at[block(4), high], half.at[q, 1], ss.at[q, 7], sr.at[q, 7], z_peer(-2))
        send(buf.at[block(1), r], recv.at[q, 0], ss.at[q, 0], sr.at[q, 0], z_peer(1))
        send(buf.at[block(-1), r], recv.at[q, 1], ss.at[q, 1], sr.at[q, 1], z_peer(-1))

    def z_second(q, buf, recv, half, ss, sr):
        r = rows_of(q)
        for n, way in ((0, 2), (1, -2)):
            arrived(recv.at[q, 2 + n], ss.at[q, 2 + n], sr.at[q, 2 + n])
            arrived(half.at[q, n], ss.at[q, 6 + n], sr.at[q, 6 + n])
            total = buf[block(way), r].astype(F32) + recv[q, 2 + n].astype(F32)
            extra = half[q, n].astype(F32)
            zeros = jnp.zeros_like(extra)
            total = total + jnp.concatenate([extra, zeros] if n == 0 else [zeros, extra], axis=0)
            buf[block(way), r] = total.astype(BF16)
            send(buf.at[block(way), r], recv.at[q, 4 + n], ss.at[q, 4 + n], sr.at[q, 4 + n], z_peer(way))

    def z_total(q, own, recv, ss, sr):
        total = own
        for n in (0, 1, 4, 5):
            arrived(recv.at[q, n], ss.at[q, n], sr.at[q, n])
            total = total + recv[q, n].astype(F32)
        return total

    def b1(q):
        a[q] = share(q, 1 - c).astype(BF16)
        send(a.at[q], ar.at[q], b_s.at[q], b_r.at[q], sibling)

    def b2(q):
        both = share(q, c)
        arrived(ar.at[q], b_s.at[q], b_r.at[q])
        both = both + ar[q].astype(F32)
        af[q] = both
        ah[:, rows_of(q)] = both.astype(BF16)
        z_first(q, ah, az, azh, bz_s, bz_r)

    def b3(q):
        z_second(q, ah, az, azh, bz_s, bz_r)

    def c1(q):
        if q == 0:
            loads[5].wait()
        r = rows_of(q)
        stream = res_v[r].astype(F32) + z_total(q, af[q, z], az, bz_s, bz_r)
        st[z, r] = stream.astype(BF16)
        mine = st.at[z, r]
        for n, way in ((2, 2), (3, -2), (0, 1), (1, -1)):
            send(mine, mine, cz_s.at[q, n], cz_r.at[q, n], z_peer(way))

    def c2(q):
        r = rows_of(q)
        low, high = pl.ds(R * q, R // 2), pl.ds(R * q + R // 2, R // 2)
        mine = st.at[z, r]
        for n, way, part in ((0, 1, low), (1, -1, high)):
            arrived(mine, cz_s.at[q, 2 + n], cz_r.at[q, 2 + n])
            far = block(-2 * way)
            send(st.at[far, r], st.at[far, r], cz_s.at[q, 4 + n], cz_r.at[q, 4 + n], z_peer(way))
            send(st.at[far, part], st.at[far, part], cz_s.at[q, 6 + n], cz_r.at[q, 6 + n], z_peer(2 * way))

    def cube(order, step, flip):
        at = [slice(None)] * 4
        for n in range(step):
            at[order[n]] = bits[order[n]]
        at[order[step]] = 1 - bits[order[step]] if flip else bits[order[step]]
        return tuple(at)

    def at_chunk(u, i):
        return (2 * u[0] + u[1], i)

    def d_lanes(u, i):
        lo, hi = D_TILES[u[1]][i]
        return (slice(None), pl.ds(0, 128 * (hi - lo)))

    def d_send(u, i, step):
        order = ORDERS[i]
        where = at_chunk(u, i) + cube(order, step, True) + d_lanes(u, i)
        if step > 0:
            total = p[where].astype(F32) + r1[where].astype(F32)
            p[where] = total.astype(BF16)
        sem = at_chunk(u, i) + (step,)
        send(p.at[where], rs[step].at[where], d_s.at[sem], d_r.at[sem], near[order[step]])

    def d_arrived(u, i, step):
        where = at_chunk(u, i) + cube(ORDERS[i], step, False) + d_lanes(u, i)
        sem = at_chunk(u, i) + (step,)
        arrived(rs[step].at[where], d_s.at[sem], d_r.at[sem])

    def d1(u):
        q, units = u
        if u == (0, 1):
            arrived(gu_v.at[0], w_s.at[0], w_r.at[0])
        if units == 0:
            r = rows_of(q)
            mine = st.at[z, r]
            for n in (0, 1, 4, 5):
                arrived(mine, cz_s.at[q, n], cz_r.at[q, n])
            for n in (6, 7):
                arrived(st.at[z, pl.ds(R * q, R // 2)], cz_s.at[q, n], cz_r.at[q, n])
            wide = st[:, r].reshape(8 * R, W).astype(F32)
            scaled = (wide * gain[...].astype(F32).reshape(1, W)).astype(BF16)
            sc[q] = scaled.reshape(2, 2, 2, 2, RD, W)
            squares = jnp.sum(wide * wide, axis=1, keepdims=True)
            lane = lax.broadcasted_iota(jnp.int32, (8 * R, 128), 1)
            row = lax.broadcasted_iota(jnp.int32, (8 * R, 128), 0) % RD
            sq[q, 0] = jnp.where(lane == row, squares, 0.0).reshape(16, RD, 128).sum(axis=1)
            for k in (1, 3, 2):
                send(sq.at[q, 0], sqx.at[q, k], q_s.at[q, 0, k], q_r.at[q, 0, k], x_peer(k))

        for sent in (True, False):
            for i in range(4):
                lo, hi = D_TILES[units][i]
                width = 128 * (hi - lo)
                half = cube(ORDERS[i], 0, sent)
                part = dot(sc[(q,) + half].reshape(8 * RD, W), gu_v[units, :, 128 * lo:128 * hi]).astype(BF16)
                p[at_chunk(u, i) + half + (slice(None), slice(0, width))] = part.reshape(2, 2, 2, RD, width)
                if sent:
                    d_send(u, i, 0)

    def d2(u):
        q, units = u
        if units == 0:
            total = sq[q, 0]
            for k in (1, 3, 2):
                arrived(sqx.at[q, k], q_s.at[q, 0, k], q_r.at[q, 0, k])
                total = total + sqx[q, k]
            sq[q, 1] = total
            for k in (1, 3, 2):
                send(sq.at[q, 1], sqy.at[q, k], q_s.at[q, 1, k], q_r.at[q, 1, k], y_peer(k))
        for i in range(4):
            d_arrived(u, i, 0)
            d_send(u, i, 1)

    def last_axis(i):
        return (x_peer, x, (2, 3)) if ORDERS[i][0] < 2 else (y_peer, y, (0, 1))

    def bits_at(i, k):
        _, at, dims = last_axis(i)
        there = (at + k) % 4
        full = list(bits)
        full[dims[0]], full[dims[1]] = there // 2, (there + there // 2) % 2
        return tuple(full)

    def d3(u):
        for i in range(4):
            d_arrived(u, i, 1)
            for k in (2, 1, 3):
                where = at_chunk(u, i) + bits_at(i, k) + d_lanes(u, i)
                total = p[where].astype(F32) + r1[where].astype(F32) + r2[where].astype(F32)
                p[where] = total.astype(BF16)
                sem = at_chunk(u, i) + (1 + k,)
                send(p.at[where], r3.at[at_chunk(u, i) + (k,) + d_lanes(u, i)], d_s.at[sem], d_r.at[sem], last_axis(i)[0](k))

    def h_ref(u, i, at):
        lo, hi = E_TILES[u[1]][i]
        return hs[i].at[(2 * u[0] + u[1],) + tuple(at) + (slice(None), pl.ds(0, 128 * (hi - lo)))]

    def d4(u):
        q, units = u
        if units == 0:
            squares = sq[q, 1]
            for k in (1, 3, 2):
                arrived(sqy.at[q, k], q_s.at[q, 1, k], q_r.at[q, 1, k])
                squares = squares + sqy[q, k]
            here = 8 * bits[0] + 4 * bits[1] + 2 * bits[2] + bits[3]
            row = lax.broadcasted_iota(jnp.int32, (16, 128), 0)
            squares = jnp.sum(jnp.where(row == here, squares, 0.0), axis=0, keepdims=True)
            row = lax.broadcasted_iota(jnp.int32, (RD, 128), 0)
            lane = lax.broadcasted_iota(jnp.int32, (RD, 128), 1)
            squares = jnp.sum(jnp.where(row == lane, squares, 0.0), axis=1, keepdims=True)
            inv[q] = jnp.broadcast_to(lax.rsqrt(squares / D + EPS), (RD, 128))
        tiles = []
        for i in range(4):
            at = at_chunk(u, i) + tuple(bits) + d_lanes(u, i)
            total = p[at].astype(F32) + r1[at].astype(F32) + r2[at].astype(F32)
            for k in (1, 3, 2):
                at = at_chunk(u, i) + (k,) + d_lanes(u, i)
                sem = at_chunk(u, i) + (1 + k,)
                arrived(r3.at[at], d_s.at[sem], d_r.at[sem])
                total = total + r3[at].astype(F32)
            lo, hi = D_TILES[units][i]
            tiles += [total[:, 128 * n:128 * n + 128] for n in range(hi - lo)]
        inverse = inv[q]
        for i in range(4):
            lo, hi = E_TILES[units][i]
            for n in range(lo, hi):
                gate, up = tiles[n] * inverse, tiles[7 + n] * inverse
                hidden = gate / (1.0 + jnp.exp(-gate)) * up
                hs[i][(2 * q + units,) + tuple(bits) + (slice(None), slice(128 * (n - lo), 128 * (n - lo) + 128))] = hidden.astype(BF16)
            ref = h_ref(u, i, bits)
            for k in (2, 1, 3):
                sem = at_chunk(u, i) + (k - 1,)
                send(ref, ref, e_s.at[sem], e_r.at[sem], last_axis(i)[0](k))

    def e_at(i, step):
        order = ORDERS[i]
        at = [slice(None)] * 4
        for n in range(2 - step):
            at[order[n]] = bits[order[n]]
        return at

    def e_send(u, i, step):
        ref = h_ref(u, i, e_at(i, step))
        sem = at_chunk(u, i) + (3 + step,)
        send(ref, ref, e_s.at[sem], e_r.at[sem], near[ORDERS[i][1 - step]])

    def e_arrived(u, i, step):
        at = e_at(i, step)
        dim = ORDERS[i][1 - step]
        at[dim] = 1 - bits[dim]
        sem = at_chunk(u, i) + (3 + step,)
        arrived(h_ref(u, i, at), e_s.at[sem], e_r.at[sem])

    def e2(u):
        for i in range(4):
            ref = h_ref(u, i, bits)
            for k in (1, 3, 2):
                sem = at_chunk(u, i) + (k - 1,)
                arrived(ref, e_s.at[sem], e_r.at[sem])
            e_send(u, i, 0)

    def e3(u):
        for i in range(4):
            e_arrived(u, i, 0)
            e_send(u, i, 1)

    def f1(q):
        if q == 0:
            arrived(dw_v.at[1], w_s.at[1], w_r.at[1])
        total = None
        for units in (0, 1):
            for i in range(4):
                e_arrived((q, units), i, 1)
                lo, hi = E_TILES[units][i]
                rows = hs[i][2 * q + units, :, :, :, :, :, 0:128 * (hi - lo)].reshape(8 * R, 128 * (hi - lo))
                part = dot(rows, dw_v[units, 128 * lo:128 * hi])
                total = part if total is None else total + part
        f[:, rows_of(q)] = total.astype(BF16).reshape(8, R, W)
        z_first(q, f, fz, fzh, fz_s, fz_r)

    def f2(q):
        z_second(q, f, fz, fzh, fz_s, fz_r)

    def f3(q):
        r = rows_of(q)
        total = z_total(q, f[z, r].astype(F32), fz, fz_s, fz_r)
        out[r] = (st[z, r].astype(F32) + total).astype(BF16)

    parts = list(range(NQ))
    chunks = [(q, units) for q in parts for units in (0, 1)]
    for stage in (b1, b2):
        for q in parts:
            stage(q)
    loads[2].wait()
    gu_v[0, :, 0:FF] = gu_in[:, 0, :]
    for q in parts:
        b3(q)
    gu_v[0, :, FF:2 * FF] = gu_in[:, 1, :]
    send(gu_v.at[0], gu_v.at[1], w_s.at[0], w_r.at[0], sibling)
    for stage in (c1, c2):
        for q in parts:
            stage(q)
    for stage in (d1, d2, d3, d4, e2, e3):
        for u in chunks:
            stage(u)
    for stage in (f1, f2, f3):
        for q in parts:
            stage(q)
    for cp in sends:
        cp.wait_send()


def local(head_out, residual, class_ids, head_mask, out_weight, norm_gain, gate_up, down_weight):
    hbm = pl.BlockSpec(memory_space=pl.ANY)
    vmem = pl.BlockSpec(memory_space=pltpu.VMEM)
    smem = pl.BlockSpec(memory_space=pltpu.SMEM)
    dma = pltpu.SemaphoreType.DMA
    cube = (2 * NQ, 4, 2, 2, 2, 2, RD, 512)
    return pl.pallas_call(
        kernel,
        out_shape=jax.ShapeDtypeStruct((64, W), BF16),
        in_specs=[hbm, hbm, vmem, smem, hbm, vmem, hbm, hbm],
        out_specs=vmem,
        scratch_shapes=[
            pltpu.VMEM((W, W), BF16),
            pltpu.VMEM((W, 2, FF), BF16),
            pltpu.VMEM((2, W, 2 * FF), BF16),
            pltpu.VMEM((2, FF, W), BF16),
            pltpu.VMEM((64, W), BF16),
            pltpu.VMEM((2, 8, 2, 64, 256), BF16),
            pltpu.VMEM((CLASSES, TOKENS), BF16),
            pltpu.VMEM((8, 2, 64, CLASSES), BF16),
            pltpu.VMEM((2, CLASSES, 256), BF16),
            pltpu.VMEM((NQ, 8, R, W), BF16),
            pltpu.VMEM((NQ, 8, R, W), BF16),
            pltpu.VMEM((NQ, 8, R, W), F32),
            pltpu.VMEM((NQ, 6, R, W), BF16),
            pltpu.VMEM((NQ, 2, R // 2, W), BF16),
            pltpu.VMEM((8, 64, W), BF16),
            pltpu.VMEM((8, 64, W), BF16),
            pltpu.VMEM((NQ, 2, 2, 2, 2, RD, W), BF16),
            pltpu.VMEM((NQ, RD, 128), F32),
            pltpu.VMEM((NQ, 2, 16, 128), F32),
            pltpu.VMEM((NQ, 4, 16, 128), F32),
            pltpu.VMEM((NQ, 4, 16, 128), F32),
            *[pltpu.VMEM(cube, BF16) for _ in range(3)],
            pltpu.VMEM((2 * NQ, 4, 4, RD, 512), BF16),
            *[pltpu.VMEM((2 * NQ, 2, 2, 2, 2, RD, 256), BF16) for _ in range(4)],
            pltpu.VMEM((8, 64, W), BF16),
            pltpu.VMEM((NQ, 6, R, W), BF16),
            pltpu.VMEM((NQ, 2, R // 2, W), BF16),
            dma((6,)),
            dma((2,)), dma((2,)),
            dma((2, 4)), dma((2, 4)),
            dma((2, 4, 4)), dma((2, 4, 4)),
            dma((NQ,)), dma((NQ,)),
            dma((NQ, 8)), dma((NQ, 8)),
            dma((NQ, 8)), dma((NQ, 8)),
            dma((2 * NQ, 4, 5)), dma((2 * NQ, 4, 5)),
            dma((NQ, 2, 4)), dma((NQ, 2, 4)),
            dma((2 * NQ, 4, 5)), dma((2 * NQ, 4, 5)),
            dma((NQ, 8)), dma((NQ, 8)),
        ],
        compiler_params=pltpu.CompilerParams(
            collective_id=0, has_side_effects=True, vmem_limit_bytes=56 << 20
        ),
        name="layer",
    )(head_out, residual, class_ids.reshape(1, TOKENS), head_mask, out_weight, norm_gain,
      gate_up, down_weight)


def solution(mesh):
    in_specs = (
        P("dp", "tensor"),
        P("tensor", "dp"),
        P(),
        P("tensor"),
        P("tensor", "dp"),
        P("dp"),
        P("dp", None, "tensor"),
        P("tensor", "dp"),
    )
    return jax.shard_map(local, mesh=mesh, in_specs=in_specs, out_specs=P("tensor", "dp"), check_vma=False)
```

```python
import jax
import jax.numpy as jnp
from jax import lax
from jax.experimental import pallas as pl
from jax.experimental.pallas import tpu as pltpu
from jax.sharding import PartitionSpec as P

MESH = pl.DeviceIdType.MESH
BF16 = jnp.bfloat16
F32 = jnp.float32
D = 8192
HEAD_DIM = 128
CLASSES = 256
EPS = 1e-05
TOKENS = 1024
W = 512
FF = 896
NQ = 2
R = 64 // NQ
RD = R // 2
ORDERS = ((3, 2, 1, 0), (2, 3, 0, 1), (1, 0, 3, 2), (0, 1, 2, 3))
D_TILES = (((0, 4), (4, 8), (8, 11), (11, 14)), ((0, 3), (3, 6), (6, 10), (10, 14)))
E_TILES = (((0, 2), (2, 4), (4, 6), (6, 7)), ((0, 1), (1, 3), (3, 5), (5, 7)))


def dot(a, b):
    return jnp.dot(a, b, preferred_element_type=F32)


def kernel(ho, res, ids, mask, ow, gain, gu, dw, out,
           ow_v, gu_in, gu_v, dw_v, res_v, g, oh, oht, mean, a, ar, af, az, azh, ah, st, sc, inv, sq, sqx, sqy, p, r1, r2, r3, h0, h1, h2, h3, f, fz, fzh,
           load_sem, w_s, w_r, x_s, x_r, a_s, a_r, b_s, b_r, bz_s, bz_r, cz_s, cz_r, d_s, d_r, q_s, q_r, e_s, e_r, fz_s, fz_r):
    dp = lax.axis_index("dp")
    tn = lax.axis_index("tensor")
    y, x = dp // 4, dp % 4
    z, c = tn // 2, tn % 2
    rs = (r1, r2)
    hs = (h0, h1, h2, h3)
    bits = (y // 2, (y + y // 2) % 2, x // 2, (x + x // 2) % 2)
    near = (
        ((3 - y) * 4 + x, tn),
        ((y + 1 - 2 * (y % 2)) * 4 + x, tn),
        (y * 4 + 3 - x, tn),
        (y * 4 + x + 1 - 2 * (x % 2), tn),
    )
    sibling = (dp, z * 2 + 1 - c)

    def x_peer(k):
        return (y * 4 + (x + k) % 4, tn)

    def y_peer(k):
        return (((y + k) % 4) * 4 + x, tn)

    def z_peer(k):
        return (dp, ((z + k + 8) % 8) * 2 + c)

    def block(k):
        return (z + k + 8) % 8

    sends = []

    def send(src, dst, ssem, rsem, to):
        cp = pltpu.make_async_remote_copy(src_ref=src, dst_ref=dst, send_sem=ssem, recv_sem=rsem,
                                          device_id=to, device_id_type=MESH)
        cp.start()
        sends.append(cp)

    def arrived(ref, ssem, rsem):
        while len(sends) > 48:
            sends.pop(0).wait_send()
        pltpu.make_async_remote_copy(src_ref=ref, dst_ref=ref, send_sem=ssem, recv_sem=rsem,
                                     device_id=sibling, device_id_type=MESH).wait_recv()

    loads = [
        pltpu.make_async_copy(ho.at[:, 0:256], g.at[0, dp // 2, dp % 2], load_sem.at[0]),
        pltpu.make_async_copy(ho.at[:, 256:512], g.at[1, dp // 2, dp % 2], load_sem.at[1]),
        pltpu.make_async_copy(gu, gu_in, load_sem.at[2]),
        pltpu.make_async_copy(dw, dw_v.at[0], load_sem.at[3]),
        pltpu.make_async_copy(ow, ow_v, load_sem.at[4]),
        pltpu.make_async_copy(res, res_v, load_sem.at[5]),
    ]
    for cp in loads:
        cp.start()

    barrier = pltpu.get_barrier_semaphore()
    peers = [x_peer(k) for k in (1, 2, 3)] + [y_peer(k) for k in (1, 2, 3)] + [z_peer(k) for k in (1, -1, 2, -2)] + [sibling]
    for to in peers:
        pl.semaphore_signal(barrier, inc=1, device_id=to, device_id_type=MESH)

    pl.semaphore_wait(barrier, len(peers))

    first = ((x_peer, y_peer), (y_peer, x_peer))
    mine = [ho.at[:, 256 * h:256 * h + 256] for h in (0, 1)]
    slot = [g.at[h, dp // 2, dp % 2] for h in (0, 1)]
    for k in (1, 3, 2):
        for h in (0, 1):
            send(mine[h], slot[h], x_s.at[h, k], x_r.at[h, k], first[h][0](k))
    for k in (1, 3, 2):
        for h in (0, 1):
            send(mine[h], slot[h], a_s.at[h, 0, k], a_r.at[h, 0, k], first[h][1](k))
    loads[3].wait()
    send(dw_v.at[0], dw_v.at[1], w_s.at[1], w_r.at[1], sibling)
    same = lax.broadcasted_iota(jnp.int32, (CLASSES, TOKENS), 0) == ids[...]
    onehot = same.astype(F32)
    counts = jnp.sum(onehot, axis=1, keepdims=True)
    oh[...] = onehot.astype(BF16)
    for j in (1, 3, 2):
        for h in (0, 1):
            source = y * 4 + (x - j + 4) % 4 if h == 0 else (y - j + 4) % 4 * 4 + x
            got = g.at[h, source // 2, source % 2]
            arrived(got, x_s.at[h, j], x_r.at[h, j])
            for k in (1, 3, 2):
                send(got, got, a_s.at[h, j, k], a_r.at[h, j, k], first[h][1](k))
    oht[...] = onehot.T.astype(BF16).reshape(8, 2, 64, CLASSES)
    for j in range(4):
        for k in (1, 2, 3):
            for h in (0, 1):
                arrived(slot[h], a_s.at[h, j, k], a_r.at[h, j, k])

    loads[0].wait()
    loads[1].wait()

    for h in (0, 1):
        totals = dot(oh[...], g[h].reshape(TOKENS, 256))
        mean[h] = (totals / jnp.maximum(counts, 1.0)).astype(BF16)
    lane_head = lax.broadcasted_iota(jnp.int32, (1, 256), 1) // HEAD_DIM
    ablate = [jnp.where(lane_head == 0, mask[2 * h], mask[2 * h + 1]) == 1 for h in (0, 1)]
    loads[4].wait()

    def share(q, core):
        rows = oht[:, core, rows_of(q)].reshape(8 * R, CLASSES)
        total = None
        for h in (0, 1):
            looked = dot(rows, mean[h])
            kept = g[h, :, core, rows_of(q)].reshape(8 * R, 256).astype(F32)
            patched = jnp.where(ablate[h], looked, kept).astype(BF16)
            part = dot(patched, ow_v[256 * h:256 * h + 256])
            total = part if total is None else total + part
        return total.reshape(8, R, W)

    def rows_of(q):
        return pl.ds(R * q, R)

    def z_first(q, buf, recv, half, ss, sr):
        r = rows_of(q)
        low, high = pl.ds(R * q, R // 2), pl.ds(R * q + R // 2, R // 2)
        send(buf.at[block(3), r], recv.at[q, 2], ss.at[q, 2], sr.at[q, 2], z_peer(1))
        send(buf.at[block(-3), r], recv.at[q, 3], ss.at[q, 3], sr.at[q, 3], z_peer(-1))
        send(buf.at[block(4), low], half.at[q, 0], ss.at[q, 6], sr.at[q, 6], z_peer(2))
        send(buf.at[block(4), high], half.at[q, 1], ss.at[q, 7], sr.at[q, 7], z_peer(-2))
        send(buf.at[block(1), r], recv.at[q, 0], ss.at[q, 0], sr.at[q, 0], z_peer(1))
        send(buf.at[block(-1), r], recv.at[q, 1], ss.at[q, 1], sr.at[q, 1], z_peer(-1))

    def z_second(q, buf, recv, half, ss, sr):
        r = rows_of(q)
        for n, way in ((0, 2), (1, -2)):
            arrived(recv.at[q, 2 + n], ss.at[q, 2 + n], sr.at[q, 2 + n])
            arrived(half.at[q, n], ss.at[q, 6 + n], sr.at[q, 6 + n])
            total = buf[block(way), r].astype(F32) + recv[q, 2 + n].astype(F32)
            extra = half[q, n].astype(F32)
            zeros = jnp.zeros_like(extra)
            total = total + jnp.concatenate([extra, zeros] if n == 0 else [zeros, extra], axis=0)
            buf[block(way), r] = total.astype(BF16)
            send(buf.at[block(way), r], recv.at[q, 4 + n], ss.at[q, 4 + n], sr.at[q, 4 + n], z_peer(way))

    def z_total(q, own, recv, ss, sr):
        total = own
        for n in (0, 1, 4, 5):
            arrived(recv.at[q, n], ss.at[q, n], sr.at[q, n])
            total = total + recv[q, n].astype(F32)
        return total

    def b1(q):
        a[q] = share(q, 1 - c).astype(BF16)
        send(a.at[q], ar.at[q], b_s.at[q], b_r.at[q], sibling)

    def b2(q):
        both = share(q, c)
        arrived(ar.at[q], b_s.at[q], b_r.at[q])
        both = both + ar[q].astype(F32)
        af[q] = both
        ah[:, rows_of(q)] = both.astype(BF16)
        z_first(q, ah, az, azh, bz_s, bz_r)

    def b3(q):
        z_second(q, ah, az, azh, bz_s, bz_r)

    def c1(q):
        if q == 0:
            loads[5].wait()
        r = rows_of(q)
        stream = res_v[r].astype(F32) + z_total(q, af[q, z], az, bz_s, bz_r)
        st[z, r] = stream.astype(BF16)
        mine = st.at[z, r]
        for n, way in ((2, 2), (3, -2), (0, 1), (1, -1)):
            send(mine, mine, cz_s.at[q, n], cz_r.at[q, n], z_peer(way))

    def c2(q):
        r = rows_of(q)
        low, high = pl.ds(R * q, R // 2), pl.ds(R * q + R // 2, R // 2)
        mine = st.at[z, r]
        for n, way, part in ((0, 1, low), (1, -1, high)):
            arrived(mine, cz_s.at[q, 2 + n], cz_r.at[q, 2 + n])
            far = block(-2 * way)
            send(st.at[far, r], st.at[far, r], cz_s.at[q, 4 + n], cz_r.at[q, 4 + n], z_peer(way))
            send(st.at[far, part], st.at[far, part], cz_s.at[q, 6 + n], cz_r.at[q, 6 + n], z_peer(2 * way))

    def cube(order, step, flip):
        at = [slice(None)] * 4
        for n in range(step):
            at[order[n]] = bits[order[n]]
        at[order[step]] = 1 - bits[order[step]] if flip else bits[order[step]]
        return tuple(at)

    def at_chunk(u, i):
        return (2 * u[0] + u[1], i)

    def d_lanes(u, i):
        lo, hi = D_TILES[u[1]][i]
        return (slice(None), pl.ds(0, 128 * (hi - lo)))

    def d_send(u, i, step):
        order = ORDERS[i]
        where = at_chunk(u, i) + cube(order, step, True) + d_lanes(u, i)
        if step > 0:
            total = p[where].astype(F32) + r1[where].astype(F32)
            p[where] = total.astype(BF16)
        sem = at_chunk(u, i) + (step,)
        send(p.at[where], rs[step].at[where], d_s.at[sem], d_r.at[sem], near[order[step]])

    def d_arrived(u, i, step):
        where = at_chunk(u, i) + cube(ORDERS[i], step, False) + d_lanes(u, i)
        sem = at_chunk(u, i) + (step,)
        arrived(rs[step].at[where], d_s.at[sem], d_r.at[sem])

    def d1(u):
        q, units = u
        if u == (0, 1):
            arrived(gu_v.at[0], w_s.at[0], w_r.at[0])
        if units == 0:
            r = rows_of(q)
            mine = st.at[z, r]
            for n in (0, 1, 4, 5):
                arrived(mine, cz_s.at[q, n], cz_r.at[q, n])
            for n in (6, 7):
                arrived(st.at[z, pl.ds(R * q, R // 2)], cz_s.at[q, n], cz_r.at[q, n])
            wide = st[:, r].reshape(8 * R, W).astype(F32)
            scaled = (wide * gain[...].astype(F32).reshape(1, W)).astype(BF16)
            sc[q] = scaled.reshape(2, 2, 2, 2, RD, W)
            squares = jnp.sum(wide * wide, axis=1, keepdims=True)
            lane = lax.broadcasted_iota(jnp.int32, (8 * R, 128), 1)
            row = lax.broadcasted_iota(jnp.int32, (8 * R, 128), 0) % RD
            sq[q, 0] = jnp.where(lane == row, squares, 0.0).reshape(16, RD, 128).sum(axis=1)
            for k in (1, 3, 2):
                send(sq.at[q, 0], sqx.at[q, k], q_s.at[q, 0, k], q_r.at[q, 0, k], x_peer(k))

        for sent in (True, False):
            for i in range(4):
                lo, hi = D_TILES[units][i]
                width = 128 * (hi - lo)
                half = cube(ORDERS[i], 0, sent)
                part = dot(sc[(q,) + half].reshape(8 * RD, W), gu_v[units, :, 128 * lo:128 * hi]).astype(BF16)
                p[at_chunk(u, i) + half + (slice(None), slice(0, width))] = part.reshape(2, 2, 2, RD, width)
                if sent:
                    d_send(u, i, 0)

    def d2(u):
        q, units = u
        if units == 0:
            total = sq[q, 0]
            for k in (1, 3, 2):
                arrived(sqx.at[q, k], q_s.at[q, 0, k], q_r.at[q, 0, k])
                total = total + sqx[q, k]
            sq[q, 1] = total
            for k in (1, 3, 2):
                send(sq.at[q, 1], sqy.at[q, k], q_s.at[q, 1, k], q_r.at[q, 1, k], y_peer(k))
        for i in range(4):
            d_arrived(u, i, 0)
            d_send(u, i, 1)

    def last_axis(i):
        return (x_peer, x, (2, 3)) if ORDERS[i][0] < 2 else (y_peer, y, (0, 1))

    def bits_at(i, k):
        _, at, dims = last_axis(i)
        there = (at + k) % 4
        full = list(bits)
        full[dims[0]], full[dims[1]] = there // 2, (there + there // 2) % 2
        return tuple(full)

    def d3(u):
        for i in range(4):
            d_arrived(u, i, 1)
            for k in (1, 3, 2):
                where = at_chunk(u, i) + bits_at(i, k) + d_lanes(u, i)
                total = p[where].astype(F32) + r1[where].astype(F32) + r2[where].astype(F32)
                p[where] = total.astype(BF16)
                sem = at_chunk(u, i) + (1 + k,)
                send(p.at[where], r3.at[at_chunk(u, i) + (k,) + d_lanes(u, i)], d_s.at[sem], d_r.at[sem], last_axis(i)[0](k))

    def h_ref(u, i, at):
        lo, hi = E_TILES[u[1]][i]
        return hs[i].at[(2 * u[0] + u[1],) + tuple(at) + (slice(None), pl.ds(0, 128 * (hi - lo)))]

    def d4(u):
        q, units = u
        if units == 0:
            squares = sq[q, 1]
            for k in (1, 3, 2):
                arrived(sqy.at[q, k], q_s.at[q, 1, k], q_r.at[q, 1, k])
                squares = squares + sqy[q, k]
            here = 8 * bits[0] + 4 * bits[1] + 2 * bits[2] + bits[3]
            row = lax.broadcasted_iota(jnp.int32, (16, 128), 0)
            squares = jnp.sum(jnp.where(row == here, squares, 0.0), axis=0, keepdims=True)
            row = lax.broadcasted_iota(jnp.int32, (RD, 128), 0)
            lane = lax.broadcasted_iota(jnp.int32, (RD, 128), 1)
            squares = jnp.sum(jnp.where(row == lane, squares, 0.0), axis=1, keepdims=True)
            inv[q] = jnp.broadcast_to(lax.rsqrt(squares / D + EPS), (RD, 128))
        tiles = []
        for i in range(4):
            at = at_chunk(u, i) + tuple(bits) + d_lanes(u, i)
            total = p[at].astype(F32) + r1[at].astype(F32) + r2[at].astype(F32)
            for k in (1, 3, 2):
                at = at_chunk(u, i) + (k,) + d_lanes(u, i)
                sem = at_chunk(u, i) + (1 + k,)
                arrived(r3.at[at], d_s.at[sem], d_r.at[sem])
                total = total + r3[at].astype(F32)
            lo, hi = D_TILES[units][i]
            tiles += [total[:, 128 * n:128 * n + 128] for n in range(hi - lo)]
        inverse = inv[q]
        for i in range(4):
            lo, hi = E_TILES[units][i]
            for n in range(lo, hi):
                gate, up = tiles[n] * inverse, tiles[7 + n] * inverse
                hidden = gate / (1.0 + jnp.exp(-gate)) * up
                hs[i][(2 * q + units,) + tuple(bits) + (slice(None), slice(128 * (n - lo), 128 * (n - lo) + 128))] = hidden.astype(BF16)
            ref = h_ref(u, i, bits)
            for k in (1, 3, 2):
                sem = at_chunk(u, i) + (k - 1,)
                send(ref, ref, e_s.at[sem], e_r.at[sem], last_axis(i)[0](k))

    def e_at(i, step):
        order = ORDERS[i]
        at = [slice(None)] * 4
        for n in range(2 - step):
            at[order[n]] = bits[order[n]]
        return at

    def e_send(u, i, step):
        ref = h_ref(u, i, e_at(i, step))
        sem = at_chunk(u, i) + (3 + step,)
        send(ref, ref, e_s.at[sem], e_r.at[sem], near[ORDERS[i][1 - step]])

    def e_arrived(u, i, step):
        at = e_at(i, step)
        dim = ORDERS[i][1 - step]
        at[dim] = 1 - bits[dim]
        sem = at_chunk(u, i) + (3 + step,)
        arrived(h_ref(u, i, at), e_s.at[sem], e_r.at[sem])

    def e2(u):
        for i in range(4):
            ref = h_ref(u, i, bits)
            for k in (1, 3, 2):
                sem = at_chunk(u, i) + (k - 1,)
                arrived(ref, e_s.at[sem], e_r.at[sem])
            e_send(u, i, 0)

    def e3(u):
        for i in range(4):
            e_arrived(u, i, 0)
            e_send(u, i, 1)

    def f1(q):
        if q == 0:
            arrived(dw_v.at[1], w_s.at[1], w_r.at[1])
        total = None
        for units in (0, 1):
            for i in range(4):
                e_arrived((q, units), i, 1)
                lo, hi = E_TILES[units][i]
                rows = hs[i][2 * q + units, :, :, :, :, :, 0:128 * (hi - lo)].reshape(8 * R, 128 * (hi - lo))
                part = dot(rows, dw_v[units, 128 * lo:128 * hi])
                total = part if total is None else total + part
        f[:, rows_of(q)] = total.astype(BF16).reshape(8, R, W)
        z_first(q, f, fz, fzh, fz_s, fz_r)

    def f2(q):
        z_second(q, f, fz, fzh, fz_s, fz_r)

    def f3(q):
        r = rows_of(q)
        total = z_total(q, f[z, r].astype(F32), fz, fz_s, fz_r)
        out[r] = (st[z, r].astype(F32) + total).astype(BF16)

    parts = list(range(NQ))
    chunks = [(q, units) for q in parts for units in (0, 1)]
    for stage in (b1, b2):
        for q in parts:
            stage(q)
    loads[2].wait()
    gu_v[0, :, 0:FF] = gu_in[:, 0, :]
    for q in parts:
        b3(q)
    gu_v[0, :, FF:2 * FF] = gu_in[:, 1, :]
    send(gu_v.at[0], gu_v.at[1], w_s.at[0], w_r.at[0], sibling)
    for stage in (c1, c2):
        for q in parts:
            stage(q)
    for stage in (d1, d2, d3, d4, e2, e3):
        for u in chunks:
            stage(u)
    for stage in (f1, f2, f3):
        for q in parts:
            stage(q)
    for cp in sends:
        cp.wait_send()


def local(head_out, residual, class_ids, head_mask, out_weight, norm_gain, gate_up, down_weight):
    hbm = pl.BlockSpec(memory_space=pl.ANY)
    vmem = pl.BlockSpec(memory_space=pltpu.VMEM)
    smem = pl.BlockSpec(memory_space=pltpu.SMEM)
    dma = pltpu.SemaphoreType.DMA
    cube = (2 * NQ, 4, 2, 2, 2, 2, RD, 512)
    return pl.pallas_call(
        kernel,
        out_shape=jax.ShapeDtypeStruct((64, W), BF16),
        in_specs=[hbm, hbm, vmem, smem, hbm, vmem, hbm, hbm],
        out_specs=vmem,
        scratch_shapes=[
            pltpu.VMEM((W, W), BF16),
            pltpu.VMEM((W, 2, FF), BF16),
            pltpu.VMEM((2, W, 2 * FF), BF16),
            pltpu.VMEM((2, FF, W), BF16),
            pltpu.VMEM((64, W), BF16),
            pltpu.VMEM((2, 8, 2, 64, 256), BF16),
            pltpu.VMEM((CLASSES, TOKENS), BF16),
            pltpu.VMEM((8, 2, 64, CLASSES), BF16),
            pltpu.VMEM((2, CLASSES, 256), BF16),
            pltpu.VMEM((NQ, 8, R, W), BF16),
            pltpu.VMEM((NQ, 8, R, W), BF16),
            pltpu.VMEM((NQ, 8, R, W), F32),
            pltpu.VMEM((NQ, 6, R, W), BF16),
            pltpu.VMEM((NQ, 2, R // 2, W), BF16),
            pltpu.VMEM((8, 64, W), BF16),
            pltpu.VMEM((8, 64, W), BF16),
            pltpu.VMEM((NQ, 2, 2, 2, 2, RD, W), BF16),
            pltpu.VMEM((NQ, RD, 128), F32),
            pltpu.VMEM((NQ, 2, 16, 128), F32),
            pltpu.VMEM((NQ, 4, 16, 128), F32),
            pltpu.VMEM((NQ, 4, 16, 128), F32),
            *[pltpu.VMEM(cube, BF16) for _ in range(3)],
            pltpu.VMEM((2 * NQ, 4, 4, RD, 512), BF16),
            *[pltpu.VMEM((2 * NQ, 2, 2, 2, 2, RD, 256), BF16) for _ in range(4)],
            pltpu.VMEM((8, 64, W), BF16),
            pltpu.VMEM((NQ, 6, R, W), BF16),
            pltpu.VMEM((NQ, 2, R // 2, W), BF16),
            dma((6,)),
            dma((2,)), dma((2,)),
            dma((2, 4)), dma((2, 4)),
            dma((2, 4, 4)), dma((2, 4, 4)),
            dma((NQ,)), dma((NQ,)),
            dma((NQ, 8)), dma((NQ, 8)),
            dma((NQ, 8)), dma((NQ, 8)),
            dma((2 * NQ, 4, 5)), dma((2 * NQ, 4, 5)),
            dma((NQ, 2, 4)), dma((NQ, 2, 4)),
            dma((2 * NQ, 4, 5)), dma((2 * NQ, 4, 5)),
            dma((NQ, 8)), dma((NQ, 8)),
        ],
        compiler_params=pltpu.CompilerParams(
            collective_id=0, has_side_effects=True, vmem_limit_bytes=56 << 20
        ),
        name="layer",
    )(head_out, residual, class_ids.reshape(1, TOKENS), head_mask, out_weight, norm_gain,
      gate_up, down_weight)


def solution(mesh):
    in_specs = (
        P("dp", "tensor"),
        P("tensor", "dp"),
        P(),
        P("tensor"),
        P("tensor", "dp"),
        P("dp"),
        P("dp", None, "tensor"),
        P("tensor", "dp"),
    )
    return jax.shard_map(local, mesh=mesh, in_specs=in_specs, out_specs=P("tensor", "dp"), check_vma=False)
```
